32 devices in a mesh: expert: 8 (over z, y), replica: 4 (over x, core).
Axes of the slice: x: 2, y: 2, z: 4, core: 2. Of those that a mesh axis runs over, the one named last changes fastest.
Arguments:
- tokens: bfloat16 [32768, 1024], P(('expert', 'replica')), may hold values from -6 to 6
- routes: int32 [32768, 1], P(('expert', 'replica')), may hold values from 0 to 7; in each aligned block of 1024 rows (0 to 1023, 1024 to 2047, ...) at most 256 rows name the same one
- gain_one: float32 [1024], replicated, may hold values from 0.5 to 1.5
- query_weight: bfloat16 [1024, 1024], replicated, may hold values from -0.1875 to 0.1875
- key_weight: bfloat16 [1024, 1024], replicated, may hold values from -0.1875 to 0.1875
- value_weight: bfloat16 [1024, 1024], replicated, may hold values from -0.1875 to 0.1875
- out_weight: bfloat16 [1024, 1024], replicated, may hold values from -1.5 to 1.5
- gain_two: float32 [1024], replicated, may hold values from 0.5 to 1.5
- up_weight: bfloat16 [8, 1024, 4096], P('expert'), may hold values from -0.1875 to 0.1875
- down_weight: bfloat16 [8, 4096, 1024], P('expert'), may hold values from -0.125 to 0.125
- cotangent: bfloat16 [32768, 1024], P(('expert', 'replica')), may hold values from -6 to 6
Outputs:
- output: bfloat16 [32768, 1024], P(('expert', 'replica'))
- grad_tokens: float32 [32768, 1024], P(('expert', 'replica'))
- grad_gain_one: float32 [1024], replicated
- grad_query_weight: float32 [1024, 1024], replicated
- grad_key_weight: float32 [1024, 1024], replicated
- grad_value_weight: float32 [1024, 1024], replicated
- grad_out_weight: float32 [1024, 1024], replicated
- grad_gain_two: float32 [1024], replicated
- grad_up_weight: float32 [8, 1024, 4096], P('expert')
- grad_down_weight: float32 [8, 4096, 1024], P('expert')
The draws below stay inside these ranges and needn't reach their ends.
Inputs may be any that keep to these rules, and one draw needn't show every extreme that they name: `routes`: among the 1024 tokens of one device no expert is named more than 256 times; on some devices one is named exactly 256 times.
All inputs are finite; a program needn't handle non-finite values.
Results may differ from the reference program's by a relative error of at most 0.013.
Values may be sent and summed in bfloat16 or wider, within the bound.
A program may use at most 320 MiB of HBM per device.

```python
import math
import jax
import jax.numpy as jnp
import numpy as np
from jax import lax

D = 1024
HEADS = 16
HEAD_DIM = 64
FF = 4096
TOK_DEV = 1024
CAP = 256
EXPERTS = 8
TOKENS = 32768
EXPERT_ROWS = 8192


def block_scale(rng, dims, shards, low, top_value):
    loudness, own = 1.0, jax.random.fold_in(rng, 6)
    for position, parts in shards:
        draws = jnp.exp(jax.random.uniform(jax.random.fold_in(own, position), (parts,), jnp.float32, low / len(shards), top_value / len(shards)))
        loudness = loudness * jnp.repeat(draws, dims[position] // parts).reshape([-1 if axis == position else 1 for axis in range(len(dims))])
    return loudness


def shared_out(stream_key, own, number, rows, count, top, limit, skew):
    ranking = jax.random.permutation(stream_key, count)
    packed, usual = shares(count, rows * top, limit, skew, True), shares(count, rows * top, limit, skew, False)
    places = jnp.arange(count)

    def named(tallies, rotation):
        used = int((tallies > 0).sum())
        fixed = max(1, used // 4)
        moved = fixed + (places - fixed + rotation * (used - fixed)) % max(1, count - fixed)
        return jnp.zeros((count,), jnp.int32).at[ranking[jnp.where(places < fixed, places, moved)]].set(jnp.asarray(tallies, jnp.int32))

    tallies = jnp.where(number % 4 == 0, named(packed, number // 4), named(usual, number - number // 4 - 1))
    mixed = jax.random.permutation(jax.random.fold_in(own, 3), count)
    giver, sink = mixed[0:count // 2 * 2:2], mixed[1:count // 2 * 2:2]
    slack = jnp.minimum(tallies[giver] - 1, limit - tallies[sink]) // 2
    slack = jnp.where((giver == ranking[0]) | (sink == ranking[0]) | (tallies[sink] == 0), 0, jnp.maximum(slack, 0))
    moved = jax.random.randint(jax.random.fold_in(own, 4), (count // 2,), 0, 1 << 20) % (slack + 1)
    tallies = tallies.at[giver].add(-moved).at[sink].add(moved)
    labels = jnp.searchsorted(jnp.cumsum(tallies), jnp.arange(rows * top), side="right").astype(jnp.int32)
    grid = labels.reshape(top, rows).T
    grid = grid[jax.random.permutation(jax.random.fold_in(own, 1), rows)]
    rotation = jax.random.randint(jax.random.fold_in(own, 2), (rows, 1), 0, top)
    return jnp.take_along_axis(grid, (jnp.arange(top)[None, :] + rotation) % top, axis=1)


def shares(count, total, reach, skew, full):
    weights = [(1 << 20) // math.isqrt(rank ** skew) + 1 for rank in range(1, count + 1)]
    largest = reach if full else min(reach, max(-(-total // count), total * weights[0] // sum(weights)))
    least = 1 if total - largest >= count - 1 else 0
    counts, rest = [largest] + [least] * (count - 1), total - largest - least * (count - 1)
    while rest > 0:
        movable = [i for i in range(1, count) if counts[i] < largest] or [i for i in range(1, count) if counts[i] < reach]
        pool, remaining = sum([weights[i] for i in movable]), rest
        for i in movable:
            addition = min(reach - counts[i], max(1, remaining * weights[i] // pool), rest)
            counts[i] = counts[i] + addition
            rest = rest - addition
    return np.array(counts)


def normal_values(stream_key, dims, width, most, cuts=(), held_as=jnp.bfloat16):
    result = width * jax.random.normal(stream_key, dims, jnp.float32)
    if cuts:
        result = result * block_scale(stream_key, dims, cuts, -0.22, 0.18)
    return jnp.clip(result, -most, most).astype(held_as)


def setup_inputs(seed: int = 0) -> dict:
    key_list = jax.random.split(jax.random.key(seed), 12)
    tokens = normal_values(key_list[0], (TOKENS, D), 1.0, 6.0, ((0, 32),))
    routes_keys = jax.random.split(jax.random.fold_in(key_list[1], 1), TOKENS // TOK_DEV)
    routes_turns = jax.random.permutation(jax.random.fold_in(key_list[1], 3), TOKENS // TOK_DEV)
    routes = jax.vmap(lambda own, number: shared_out(jax.random.fold_in(key_list[1], 2), own, number, TOK_DEV, EXPERTS, 1, CAP, 2))(routes_keys, routes_turns).reshape((TOKENS, 1))
    gain_one = jnp.clip(1.0 + 0.1 * jax.random.normal(key_list[2], (D,), jnp.float32), 0.5, 1.5)
    query_weight = normal_values(key_list[3], (D, D), D ** -0.5, 0.1875)
    key_weight = normal_values(key_list[4], (D, D), D ** -0.5, 0.1875)
    value_weight = normal_values(key_list[5], (D, D), D ** -0.5, 0.1875)
    out_weight = normal_values(key_list[6], (D, D), (max(D // 64, 1)) ** -0.5, 1.5)
    gain_two = jnp.clip(1.0 + 0.1 * jax.random.normal(key_list[7], (D,), jnp.float32), 0.5, 1.5)
    up_weight = normal_values(key_list[8], (EXPERTS, D, FF), D ** -0.5, 0.1875, ((0, 8),))
    down_weight = normal_values(key_list[9], (EXPERTS, FF, D), (FF // 2) ** -0.5, 0.125, ((0, 8),))
    cotangent = normal_values(key_list[10], (TOKENS, D), 1.0, 6.0, ((0, 32),))
    return {"tokens": tokens, "routes": routes, "gain_one": gain_one, "query_weight": query_weight, "key_weight": key_weight, "value_weight": value_weight, "out_weight": out_weight, "gain_two": gain_two, "up_weight": up_weight, "down_weight": down_weight, "cotangent": cotangent}


@jax.custom_vjp
def low(v):
    return lax.optimization_barrier(v.astype(jnp.bfloat16)).astype(jnp.float32)

@jax.custom_vjp
def low_back(v):
    return v

def low_keep(v):
    return (low(v), None)

def low_pass(kept, grad):
    return (grad,)

def back_keep(v):
    return (v, None)

def back_low(kept, grad):
    return (low(grad),)
low.defvjp(low_keep, low_pass)
low_back.defvjp(back_keep, back_low)

def product_hi(left, right):
    return jnp.dot(left, right, precision=lax.Precision.HIGHEST, preferred_element_type=jnp.float32)

def norm_rows(rows, gain_vec):
    average = lax.optimization_barrier(jnp.mean(rows, axis=-1, keepdims=True))
    centred = rows - average
    variance = lax.optimization_barrier(jnp.mean(centred * centred, axis=-1, keepdims=True))
    return centred * lax.rsqrt(variance + 1e-05) * gain_vec

def attend(normed, query_weight, key_weight, value_weight):
    seq_len = normed.shape[0]
    normed_low = low(normed)
    query_heads = low_back(low(product_hi(normed_low, query_weight))).reshape(seq_len, HEADS, HEAD_DIM)
    key_heads = low_back(low(product_hi(normed_low, key_weight))).reshape(seq_len, HEADS, HEAD_DIM)
    value_heads = low_back(low(product_hi(normed_low, value_weight))).reshape(seq_len, HEADS, HEAD_DIM)
    block_rows = min(512, seq_len)
    scale_factor = HEAD_DIM ** (-0.5)

    def one_block(number):
        offset = number * block_rows
        query_rows = lax.dynamic_slice_in_dim(query_heads, offset, block_rows, 0)
        scores = jnp.einsum('qhd,khd->hqk', query_rows, key_heads, precision=lax.Precision.HIGHEST)
        scores = low_back(scores * scale_factor)
        row_ids = offset + lax.broadcasted_iota(jnp.int32, (block_rows, seq_len), 0)
        col_ids = lax.broadcasted_iota(jnp.int32, (block_rows, seq_len), 1)
        scores = jnp.where((col_ids <= row_ids)[None], scores, -1e+30)
        softened = low(jax.nn.softmax(scores, axis=-1))
        return jnp.einsum('hqk,khd->qhd', softened, value_heads, precision=lax.Precision.HIGHEST)
    blocks = lax.map(jax.checkpoint(one_block), jnp.arange(seq_len // block_rows, dtype=jnp.int32))
    return blocks.reshape(seq_len, HEADS * HEAD_DIM)

def slot_positions(routes):
    chosen = routes[:, 0]
    experts_row = lax.broadcasted_iota(jnp.int32, (1, EXPERTS), 1)
    onehot = (chosen[:, None] == experts_row).astype(jnp.int32).reshape(-1, TOK_DEV, EXPERTS)
    rank_in = lax.optimization_barrier(jnp.sum(jnp.cumsum(onehot, axis=1) * onehot, axis=2)) - 1
    device_ids = lax.broadcasted_iota(jnp.int32, rank_in.shape, 0)
    slot_index = chosen.reshape(rank_in.shape) * EXPERT_ROWS + device_ids * CAP + rank_in
    return slot_index.reshape(-1).astype(jnp.int32)

def reference(tokens, routes, gain_one, query_weight, key_weight, value_weight, out_weight, gain_two, up_weight, down_weight, cotangent):
    slot_index = slot_positions(routes)

    def forward(residual, gain_a, weight_q, weight_k, weight_v, weight_o, gain_b, weight_up, weight_down):
        sequences = residual.reshape(-1, TOK_DEV, D)

        def one_sequence(rows):
            normed = norm_rows(rows, gain_a)
            attended = low_back(low(attend(normed, weight_q, weight_k, weight_v)))
            return rows + low_back(product_hi(attended, weight_o))
        hidden_state = lax.map(jax.checkpoint(one_sequence), sequences).reshape(-1, D)
        sent = low_back(low(norm_rows(hidden_state, gain_b)))
        buffer = jnp.zeros((EXPERTS * EXPERT_ROWS, D), jnp.float32).at[slot_index].set(sent)
        buffer = buffer.reshape(EXPERTS, EXPERT_ROWS, D)

        def one_expert(inputs):
            rows, up_matrix, down_matrix = inputs
            hidden_pre = low_back(product_hi(rows, up_matrix))
            activated = low(jax.nn.gelu(hidden_pre))
            return low_back(low(product_hi(activated, down_matrix)))
        results = lax.map(jax.checkpoint(one_expert), (buffer, weight_up, weight_down)).reshape(-1, D)
        return hidden_state + results[slot_index]
    primal = (tokens.astype(jnp.float32), gain_one.astype(jnp.float32), query_weight.astype(jnp.float32), key_weight.astype(jnp.float32), value_weight.astype(jnp.float32), out_weight.astype(jnp.float32), gain_two.astype(jnp.float32), up_weight.astype(jnp.float32), down_weight.astype(jnp.float32))
    output, pullback = jax.vjp(forward, *primal)
    grads = pullback(cotangent.astype(jnp.float32))
    return (output.astype(jnp.bfloat16), grads[0], grads[1], grads[2], grads[3], grads[4], grads[5], grads[6], grads[7], grads[8])
```

```python
import functools
import math

import jax
import jax.numpy as jnp
from jax import lax
from jax.experimental import pallas as pl
from jax.experimental.pallas import tpu as pltpu
from jax.sharding import PartitionSpec as P

HEAD_DIM=64
F32=jnp.float32; BF=jnp.bfloat16
MESH=pl.DeviceIdType.MESH
epsilon=1e-5
def dot(a,b): return jnp.dot(a,b,preferred_element_type=F32)
def dg(a,b,ca,cb): return lax.dot_general(a,b,(((ca,),(cb,)),((),())),preferred_element_type=F32)

def xor(a,b,count):
    total=0; step=1
    while step<count:
        x=(a//step)%2; y=(b//step)%2
        total=total+step*(x+y-2*x*y); step*=2
    return total

def norm_stats(rows):
    average=jnp.mean(rows,axis=-1,keepdims=True)
    centred=rows-average
    inverse=lax.rsqrt(jnp.mean(centred*centred,axis=-1,keepdims=True)+epsilon)
    return centred*inverse,inverse

def fwd_head(qT,kT,vT,block):
    seq=qT.shape[1]
    qs=qT*jnp.asarray(HEAD_DIM**-0.5,BF)
    k=kT.T
    outs=[]; lses=[]
    for i in range(seq//block):
        b=i*block; n=b+block
        diag=dot(k[b:n],qs[:,b:n])
        rows=lax.broadcasted_iota(jnp.int32,(block,block),0); cols=lax.broadcasted_iota(jnp.int32,(block,block),1)
        diag=jnp.where(rows<=cols,diag,-1e30)
        m=jnp.max(diag,axis=0,keepdims=True)
        if i:
            s=dot(k[:b],qs[:,b:n])
            m=jnp.maximum(m,jnp.max(s,axis=0,keepdims=True))
        p=jnp.exp(diag-m)
        l=jnp.sum(p,axis=0,keepdims=True)
        o=dot(vT[:,b:n],p.astype(BF))
        if i:
            p=jnp.exp(s-m)
            l=l+jnp.sum(p,axis=0,keepdims=True)
            o=o+dot(vT[:,:b],p.astype(BF))
        outs.append((o*(1.0/l)).astype(BF)); lses.append(m+jnp.log(l))
    return outs,lses

def onehot_rows(slot,first,count):
    ids=(lax.broadcasted_iota(jnp.int32,(count,slot.shape[1]),0)+first).astype(F32)
    return jnp.where(ids==slot,1.0,0.0).astype(BF)

def front_kernel(groups,cap,block,tok,rt,cot,g1,g2,wq,wk,wv,wo,
                 normed,q,k,v,att,lse,hid,pack,slot,cotarr,
                 cpack,n2,ssem,rsem,lsem):
    T,D=tok.shape
    R=256
    me=lax.axis_index("expert")
    barrier=pltpu.get_barrier_semaphore()
    def greet(i,c):
        pl.semaphore_signal(barrier,inc=1,device_id={"expert":xor(me,i,groups)},device_id_type=MESH)
        return c
    lax.fori_loop(1,groups,greet,0)
    routes=rt[...]
    e=jnp.where(lax.broadcasted_iota(jnp.int32,(groups,T),0)==routes,1.0,0.0)
    tri=jnp.where(lax.broadcasted_iota(jnp.int32,(T,T),0)<=lax.broadcasted_iota(jnp.int32,(T,T),1),1.0,0.0).astype(BF)
    cum=dot(e.astype(BF),tri)
    rank=jnp.sum(cum*e,axis=0,keepdims=True)-1.0
    slots=routes.astype(F32)*cap+rank
    slot[...]=slots
    pl.semaphore_wait(barrier,groups-1)
    def push(i,c):
        peer=xor(me,groups-1-i,groups)
        cpack[peer]=dot(onehot_rows(slots,peer*cap,cap),cot[...]).astype(BF)
        pltpu.make_async_remote_copy(src_ref=cpack.at[peer],dst_ref=cotarr.at[me],send_sem=ssem.at[peer],recv_sem=rsem.at[me],
            device_id={"expert":peer},device_id_type=MESH).start()
        return c
    lax.fori_loop(0,groups-1,push,0)
    cpack[me]=dot(onehot_rows(slots,me*cap,cap),cot[...]).astype(BF)
    own=pltpu.make_async_copy(cpack.at[me],cotarr.at[me],lsem)
    own.start()
    def norm_one(i,c):
        r=pl.ds(pl.multiple_of(i*R,R),R)
        u,_=norm_stats(tok[r,:].astype(F32))
        normed[r,:]=(u*g1[...]).astype(BF)
        return c
    lax.fori_loop(0,T//R,norm_one,0)
    def proj(i,c):
        s=pl.ds(pl.multiple_of(i*R,R),R)
        for w,o in ((wq,q),(wk,k),(wv,v)):
            o[s,:]=dg(w[:,s],normed[...],0,1).astype(BF)
        return c
    lax.fori_loop(0,D//R,proj,0)
    def head(h,c):
        s=pl.ds(pl.multiple_of(h*HEAD_DIM,HEAD_DIM),HEAD_DIM)
        outs,lses=fwd_head(q[s,:],k[s,:],v[s,:],block)
        att[s,:]=jnp.concatenate(outs,axis=1)
        lse[pl.ds(h,1),:]=jnp.concatenate(lses,axis=1)
        return c
    lax.fori_loop(0,D//HEAD_DIM,head,0)
    def out(i,c):
        r=pl.ds(pl.multiple_of(i*R,R),R)
        h=tok[r,:].astype(F32)+dg(att[:,r],wo[...],0,0)
        hid[r,:]=h
        u,_=norm_stats(h)
        n2[r,:]=(u*g2[...]).astype(BF)
        return c
    lax.fori_loop(0,T//R,out,0)
    def packing(i,c):
        pack[i]=dot(onehot_rows(slots,i*cap,cap),n2[...]).astype(BF)
        return c
    lax.fori_loop(0,groups,packing,0)
    own.wait()
    def finish(i,c):
        peer=xor(me,i,groups)
        pltpu.make_async_remote_copy(src_ref=cpack.at[peer],dst_ref=cotarr.at[peer],send_sem=ssem.at[peer],recv_sem=rsem.at[peer],
            device_id={"expert":peer},device_id_type=MESH).wait()
        return c
    lax.fori_loop(1,groups,finish,0)

def front(tokens,routes_row,cot,g1,g2,wq,wk,wv,wo,groups,cap,block=512):
    T,D=tokens.shape
    H=D//HEAD_DIM
    V=pl.BlockSpec(memory_space=pltpu.VMEM)
    A=pl.BlockSpec(memory_space=pl.ANY)
    sd=jax.ShapeDtypeStruct
    return pl.pallas_call(functools.partial(front_kernel,groups,cap,block),
      in_specs=[V]*9,out_specs=[V]*9+[A],
      out_shape=[sd((T,D),BF)]+[sd((D,T),BF)]*4+[sd((H,T),F32),sd((T,D),F32),sd((groups,cap,D),BF),sd((1,T),F32),sd((groups,cap,D),BF)],
      scratch_shapes=[pltpu.VMEM((groups,cap,D),BF),pltpu.VMEM((T,D),BF),pltpu.SemaphoreType.DMA((groups,)),pltpu.SemaphoreType.DMA((groups,)),pltpu.SemaphoreType.DMA],
      compiler_params=pltpu.CompilerParams(vmem_limit_bytes=60*2**20,collective_id=0,has_side_effects=True),
      name="front")(tokens,routes_row,cot,g1,g2,wq,wk,wv,wo)


F32=jnp.float32; BF=jnp.bfloat16
MESH=pl.DeviceIdType.MESH
def dot(a,b): return jnp.dot(a,b,preferred_element_type=F32)
def dg(a,b,ca,cb): return lax.dot_general(a,b,(((ca,),(cb,)),((),())),preferred_element_type=F32)
def xor(a,b,count):
    total=0; step=1
    while step<count:
        x=(a//step)%2; y=(b//step)%2
        total=total+step*(x+y-2*x*y); step*=2
    return total
SQ=math.sqrt(2/math.pi)
def gelu_pair(h):
    h2=h*h
    th=jnp.tanh(h*(SQ+SQ*0.044715*h2))
    half=0.5*(1.0+th)
    act=h*half
    slope=half+act*((1.0-th)*(SQ+3*SQ*0.044715*h2))
    return act,slope

def expert_kernel(groups,cap,pack,cotarr,up,down,gback,ret,dup,ddown,act,
                  arr,upv,downv,cotv,gpre,actb,gst,retb,stage,
                  psend,precv,gsend,grecv,wsem,retsem,actsem,stsem,tsem):
    rows=groups*cap
    D,F=upv.shape
    FT=1024
    me=lax.axis_index("expert")
    barrier=pltpu.get_barrier_semaphore()
    def greet(i,c):
        pl.semaphore_signal(barrier,inc=1,device_id={"expert":xor(me,i,groups)},device_id_type=MESH)
        return c
    lax.fori_loop(1,groups,greet,0)
    pl.semaphore_wait(barrier,groups-1)
    def at(j): return pl.ds(pl.multiple_of(j*cap,cap),cap)
    def dispatch(j,i):
        return pltpu.make_async_remote_copy(src_ref=pack.at[j],dst_ref=arr.at[at(me)],send_sem=psend.at[i],recv_sem=precv.at[i],
            device_id={"expert":j},device_id_type=MESH)
    def giveback(j,i):
        return pltpu.make_async_remote_copy(src_ref=gst.at[at(j)],dst_ref=gback.at[me],send_sem=gsend.at[i],recv_sem=grecv.at[i],
            device_id={"expert":j},device_id_type=MESH)
    half=groups//2
    def push(i,c):
        dispatch(xor(me,i,groups),i).start()
        return c
    lax.fori_loop(half,half+half//2,push,0)
    lax.fori_loop(1,half,push,0)
    own=pltpu.make_async_copy(pack.at[me],arr.at[at(me)],precv.at[0])
    own.start()
    cup=pltpu.make_async_copy(up,upv,wsem.at[0]); cup.start()
    ccot=pltpu.make_async_copy(cotarr,cotv,wsem.at[1]); ccot.start()
    cdown=pltpu.make_async_copy(down,downv,wsem.at[2]); cdown.start()
    cup.wait(); ccot.wait(); cdown.wait()
    def retcopy(j,b): return pltpu.make_async_copy(retb.at[b],ret.at[j],retsem.at[b])
    def actcopy(j,b): return pltpu.make_async_copy(actb.at[b],act.at[at(j)],actsem.at[b])
    def chunk(i,c):
        j=xor(me,i,groups)
        b=i%2
        @pl.when(i==0)
        def _(): own.wait()
        @pl.when(i>0)
        def _(): dispatch(j,i).wait_recv()
        @pl.when(i==half-1)
        def _(): lax.fori_loop(half+half//2,groups,push,0)
        @pl.when(i>=2)
        def _():
            retcopy(j,b).wait(); actcopy(j,b).wait()
        def tile(t,c):
            s=pl.ds(pl.multiple_of(t*FT,FT),FT)
            h=dot(arr[at(j),:],upv[:,s])
            g=dg(cotv[j],downv[s,:],1,1)
            a,slope=gelu_pair(h)
            actb[b,:,s]=a.astype(BF)
            gpre[at(j),s]=(g*slope).astype(BF)
            return c
        lax.fori_loop(0,F//FT,tile,0)
        gst[at(j),:]=dg(gpre[at(j),:],upv[...],1,1).astype(BF)
        @pl.when(i>0)
        def _(): giveback(j,i).start()
        @pl.when(i==0)
        def _(): pltpu.make_async_copy(gst.at[at(j)],gback.at[me],grecv.at[0]).start()
        actcopy(j,b).start()
        retb[b]=dot(actb[b],downv[...]).astype(BF)
        retcopy(j,b).start()
        return c
    lax.fori_loop(0,groups,chunk,0)
    for b in range(2):
        retcopy(0,b).wait(); actcopy(0,b).wait()
    def atile(t,b): return pltpu.make_async_copy(act.at[:,pl.ds(pl.multiple_of(t*D,D),D)],downv.at[pl.ds(b*rows,rows)],tsem.at[b])
    atile(0,0).start(); atile(1,1).start()
    S=512
    def upout(t,b): return pltpu.make_async_copy(stage.at[b],dup.at[:,pl.ds(pl.multiple_of(t*S,S),S)],stsem.at[b])
    def dup_tile(t,c):
        b=t%2
        @pl.when(t>=2)
        def _(): upout(t,b).wait()
        def part(k,c):
            r=pl.ds(pl.multiple_of(k*S,S),S)
            stage[b,r,:]=dg(arr[:,r],gpre[:,pl.ds(pl.multiple_of(t*S,S),S)],0,0).astype(BF)
            return c
        lax.fori_loop(0,D//S,part,0)
        upout(t,b).start()
        return c
    lax.fori_loop(0,F//S,dup_tile,0)
    for b in range(2): upout(b,b).wait()
    def downout(f,b): return pltpu.make_async_copy(upv.at[pl.ds(b*S,S),pl.ds(0,D)],ddown.at[pl.ds(pl.multiple_of(f*S,S),S)],stsem.at[b])
    def ddown_tile(t,c):
        tb=t%2
        atile(t,tb).wait()
        def part(p,c):
            b=p%2
            @pl.when(t*(D//S)+p>=2)
            def _(): downout(0,b).wait()
            a=downv[pl.ds(pl.multiple_of(tb*rows,rows),rows),pl.ds(pl.multiple_of(p*S,S),S)]
            upv[pl.ds(pl.multiple_of(b*S,S),S),pl.ds(0,D)]=dg(a,cotv[...].reshape(rows,D),0,0).astype(BF)
            downout(t*(D//S)+p,b).start()
            return c
        lax.fori_loop(0,D//S,part,0)
        @pl.when(t+2<F//D)
        def _(): atile(t+2,tb).start()
        return c
    lax.fori_loop(0,F//D,ddown_tile,0)
    for b in range(2): downout(b,b).wait()
    pltpu.make_async_copy(gst.at[at(me)],gback.at[me],grecv.at[0]).wait()
    def finish(i,c):
        j=xor(me,i,groups)
        dispatch(j,i).wait_send()
        giveback(j,i).wait()
        return c
    lax.fori_loop(1,groups,finish,0)

def expert(pack,cotarr,up,down):
    groups,cap,D=pack.shape
    F=up.shape[1]; rows=groups*cap
    A=pl.BlockSpec(memory_space=pl.ANY)
    sd=jax.ShapeDtypeStruct
    DMA=pltpu.SemaphoreType.DMA
    return pl.pallas_call(functools.partial(expert_kernel,groups,cap),
      in_specs=[A]*4,out_specs=[A]*5,
      out_shape=[sd((groups,cap,D),BF)]*2+[sd((D,F),BF),sd((F,D),BF),sd((rows,F),BF)],
      scratch_shapes=[pltpu.VMEM((rows,D),BF),pltpu.VMEM((D,F),BF),pltpu.VMEM((F,D),BF),pltpu.VMEM((groups,cap,D),BF),pltpu.VMEM((rows,F),BF),
         pltpu.VMEM((2,cap,F),BF),pltpu.VMEM((rows,D),BF),pltpu.VMEM((2,cap,D),BF),pltpu.VMEM((2,D,512),BF),
         DMA((groups,)),DMA((groups,)),DMA((groups,)),DMA((groups,)),DMA((3,)),DMA((2,)),DMA((2,)),DMA((2,)),DMA((2,))],
      compiler_params=pltpu.CompilerParams(vmem_limit_bytes=63*2**20,collective_id=1,has_side_effects=True),
      name="experts")(pack,cotarr,up,down)


def bwd_head(qT,kT,vT,oT,doT,lse,block):
    seq=qT.shape[1]
    scale=HEAD_DIM**-0.5
    qs=qT*jnp.asarray(scale,BF)
    q=qs.T; k=kT.T; v=vT.T; do=doT.T
    delta=jnp.sum(oT.astype(F32)*doT.astype(F32),axis=0,keepdims=True)
    count=seq//block
    dqs=[None]*count; dks=[]; dvs=[]
    for j in range(count):
        b=j*block
        kj=k[b:b+block]; vj=v[b:b+block]
        s=dot(kj,qs[:,b:])
        n=seq-b
        rows=lax.broadcasted_iota(jnp.int32,(block,n),0); cols=lax.broadcasted_iota(jnp.int32,(block,n),1)
        p=jnp.where(rows<=cols,jnp.exp(s-lse[:,b:]),0.0)
        dp=dot(vj,doT[:,b:])
        ds=(p*(dp-delta[:,b:])).astype(BF)
        dvs.append(dot(p.astype(BF),do[b:]))
        dks.append(dot(ds,q[b:]))
        c=dot(kT[:,b:b+block],ds)
        for i in range(j,count):
            part=c[:,(i-j)*block:(i-j+1)*block]
            dqs[i]=part if dqs[i] is None else dqs[i]+part
    return [(x*scale).astype(BF).T for x in dqs],[x.astype(BF) for x in dks],[x.astype(BF) for x in dvs]

def back_kernel(groups,cap,block,
        gback,ret,slot,hid,cot,tok,normed,q,k,v,att,lse,g1,g2,wq,wk,wv,wo,
        output,gtok,dw,dgain,rarr,
        vslots,vhid,vcot,vtok,vnormed,vq,vk,vv,vatt,vwq,vwk,vwv,vwo,ghl,datt,dq,dk,dv,
        isem,ssem,rsem,lsem):
    T,D=vtok.shape
    R=256
    rows=groups*cap
    me=lax.axis_index("expert")
    barrier=pltpu.get_barrier_semaphore()
    def greet(i,c):
        pl.semaphore_signal(barrier,inc=1,device_id={"expert":xor(me,i,groups)},device_id_type=MESH)
        return c
    lax.fori_loop(1,groups,greet,0)
    copies=[pltpu.make_async_copy(a,b,isem.at[i]) for i,(a,b) in enumerate(
        ((gback,vslots),(hid,vhid),(cot,vcot),(wo,vwo),(att,vatt),(q,vq),(k,vk),(v,vv),(normed,vnormed),(wq,vwq),(wk,vwk),(wv,vwv),(tok,vtok)))]
    for c in copies: c.start()
    pl.semaphore_wait(barrier,groups-1)
    def send(i):
        j=xor(me,i,groups)
        return pltpu.make_async_remote_copy(src_ref=ret.at[j],dst_ref=rarr.at[me],send_sem=ssem.at[i],recv_sem=rsem.at[i],
            device_id={"expert":j},device_id_type=MESH)
    def push(i,c):
        send(groups-i).start()
        return c
    lax.fori_loop(1,groups,push,0)
    own=pltpu.make_async_copy(ret.at[me],rarr.at[me],lsem); own.start()
    def gathered(r):
        col=jnp.broadcast_to(slot[:,r],(128,R)).T[:,:1]
        ids=lax.broadcasted_iota(jnp.int32,(R,rows),1).astype(F32)
        return dot(jnp.where(ids==col,1.0,0.0).astype(BF),vslots[...].reshape(rows,D))
    for c in copies[:3]: c.wait()
    dgain[...]=jnp.zeros_like(dgain)
    def norm_two(i,c):
        r=pl.ds(pl.multiple_of(i*R,R),R)
        gs=gathered(r)
        u,inv=norm_stats(vhid[r,:])
        m=gs*g2[...]
        dgain[1:2,:]+=jnp.sum(gs*u,axis=0,keepdims=True)
        gh=vcot[r,:].astype(F32)+inv*(m-jnp.mean(m,axis=-1,keepdims=True)-u*jnp.mean(m*u,axis=-1,keepdims=True))
        gtok[r,:]=gh
        ghl[r,:]=gh.astype(BF)
        return c
    lax.fori_loop(0,T//R,norm_two,0)
    for c in copies[3:5]: c.wait()
    def outproj(i,c):
        s=pl.ds(pl.multiple_of(i*R,R),R)
        datt[s,:]=dg(vwo[s,:],ghl[...],1,1).astype(BF)
        dw[3,s,:]=dot(vatt[s,:],ghl[...]).astype(BF)
        return c
    lax.fori_loop(0,D//R,outproj,0)
    for c in copies[5:]: c.wait()
    def pair(h,c):
        w=2*HEAD_DIM
        col=pl.ds(pl.multiple_of(h*w,w),w)
        res=[]
        for a in range(2):
            s=pl.ds(pl.multiple_of(h*w+a*HEAD_DIM,HEAD_DIM),HEAD_DIM)
            res.append(bwd_head(vq[s,:],vk[s,:],vv[s,:],vatt[s,:],datt[s,:],lse[pl.ds(2*h+a,1),:],block))
        for ref,x,y in zip((dq,dk,dv),*res):
            for i in range(T//block):
                ref[i*block:(i+1)*block,col]=jnp.concatenate([x[i],y[i]],axis=1)
        return c
    lax.fori_loop(0,D//(2*HEAD_DIM),pair,0)
    def wgrad(i,c):
        s=pl.ds(pl.multiple_of(i*R,R),R)
        for n,x in enumerate((dq,dk,dv)):
            dw[n,s,:]=dg(vnormed[:,s],x[...],0,0).astype(BF)
        return c
    lax.fori_loop(0,D//R,wgrad,0)
    def norm_one(i,c):
        r=pl.ds(pl.multiple_of(i*R,R),R)
        gn=dg(dq[r,:],vwq[...],1,1)+dg(dk[r,:],vwk[...],1,1)+dg(dv[r,:],vwv[...],1,1)
        u,inv=norm_stats(vtok[r,:].astype(F32))
        m=gn*g1[...]
        dgain[0:1,:]+=jnp.sum(gn*u,axis=0,keepdims=True)
        gtok[r,:]+=inv*(m-jnp.mean(m,axis=-1,keepdims=True)-u*jnp.mean(m*u,axis=-1,keepdims=True))
        return c
    lax.fori_loop(0,T//R,norm_one,0)
    own.wait()
    def finish(i,c):
        send(i).wait()
        return c
    lax.fori_loop(1,groups,finish,0)
    load=pltpu.make_async_copy(rarr,vslots,lsem); load.start(); load.wait()
    def final(i,c):
        r=pl.ds(pl.multiple_of(i*R,R),R)
        output[r,:]=(vhid[r,:]+gathered(r)).astype(BF)
        return c
    lax.fori_loop(0,T//R,final,0)

def back(gback,ret,slot,hid,cot,tok,normed,q,k,v,att,lse,g1,g2,wq,wk,wv,wo,block=256):
    groups,cap,D=ret.shape
    T=tok.shape[0]
    V=pl.BlockSpec(memory_space=pltpu.VMEM)
    A=pl.BlockSpec(memory_space=pl.ANY)
    sd=jax.ShapeDtypeStruct
    DMA=pltpu.SemaphoreType.DMA
    dn=(D,T)
    return pl.pallas_call(functools.partial(back_kernel,groups,cap,block),
      in_specs=[A,A,V]+[A]*8+[V]*3+[A]*4,out_specs=[V]*4+[A],
      out_shape=[sd((T,D),BF),sd((T,D),F32),sd((4,D,D),BF),sd((8,D),F32),sd((groups,cap,D),BF)],
      scratch_shapes=[pltpu.VMEM((groups,cap,D),BF),pltpu.VMEM((T,D),F32)]+[pltpu.VMEM((T,D),BF)]*3+[pltpu.VMEM((D,T),BF)]*4+[pltpu.VMEM((D,D),BF)]*4
         +[pltpu.VMEM((T,D),BF),pltpu.VMEM((D,T),BF)]+[pltpu.VMEM((T,D),BF)]*3+[DMA((13,)),DMA((groups,)),DMA((groups,)),DMA],
      compiler_params=pltpu.CompilerParams(vmem_limit_bytes=63*2**20,collective_id=2,has_side_effects=True),
      name="back")(gback,ret,slot,hid,cot,tok,normed,q,k,v,att,lse,g1,g2,wq,wk,wv,wo)


def per_device(tokens,routes,gain_one,query_weight,key_weight,value_weight,out_weight,gain_two,up_weight,down_weight,cotangent):
    T,D=tokens.shape
    groups=lax.axis_size("expert")
    cap=2*T//groups
    g1=gain_one.reshape(1,D); g2=gain_two.reshape(1,D)
    weights=(query_weight,key_weight,value_weight,out_weight)
    normed,q,k,v,att,lse,hid,pack,slot,cotarr=front(tokens,routes.reshape(1,T),cotangent,g1,g2,*weights,groups,cap)
    gback,ret,dup,ddown,_=expert(pack,cotarr,up_weight[0],down_weight[0])
    output,gtok,dw,dgain,_=back(gback,ret,slot,hid,cotangent,tokens,normed,q,k,v,att,lse,g1,g2,*weights)
    sdown=lax.psum_scatter(ddown[None],"replica",scatter_dimension=1,tiled=True)
    sup=lax.psum_scatter(dup[None],"replica",scatter_dimension=2,tiled=True)
    gdown=lax.all_gather(sdown,"replica",axis=1,tiled=True).astype(F32)
    gup=lax.all_gather(sup,"replica",axis=2,tiled=True).astype(F32)
    packed=jnp.concatenate([dw.reshape(4*D,D),dgain.astype(BF)],axis=0)
    total=lax.psum(packed,("expert","replica")).astype(F32)
    ws=[total[i*D:(i+1)*D] for i in range(4)]
    return (output,gtok,total[4*D],*ws,total[4*D+1],gup,gdown)


def solution(mesh):
    rows=P(("expert","replica"),None)
    each=P("expert",None,None)
    return jax.shard_map(per_device,mesh=mesh,
        in_specs=(rows,rows,P(),P(),P(),P(),P(),P(),each,each,rows),
        out_specs=(rows,rows,P(),P(),P(),P(),P(),P(),each,each),check_vma=False)
```

```python
import functools
import math

import jax
import jax.numpy as jnp
from jax import lax
from jax.experimental import pallas as pl
from jax.experimental.pallas import tpu as pltpu
from jax.sharding import PartitionSpec as P

HEAD_DIM=64
F32=jnp.float32; BF=jnp.bfloat16
MESH=pl.DeviceIdType.MESH
epsilon=1e-5
def dot(a,b): return jnp.dot(a,b,preferred_element_type=F32)
def dg(a,b,ca,cb): return lax.dot_general(a,b,(((ca,),(cb,)),((),())),preferred_element_type=F32)

def xor(a,b,count):
    total=0; step=1
    while step<count:
        x=(a//step)%2; y=(b//step)%2
        total=total+step*(x+y-2*x*y); step*=2
    return total

def norm_stats(rows):
    average=jnp.mean(rows,axis=-1,keepdims=True)
    centred=rows-average
    inverse=lax.rsqrt(jnp.mean(centred*centred,axis=-1,keepdims=True)+epsilon)
    return centred*inverse,inverse

def fwd_head(qT,kT,vT,block):
    seq=qT.shape[1]
    qs=qT*jnp.asarray(HEAD_DIM**-0.5,BF)
    k=kT.T
    outs=[]; lses=[]
    for i in range(seq//block):
        b=i*block; n=b+block
        diag=dot(k[b:n],qs[:,b:n])
        rows=lax.broadcasted_iota(jnp.int32,(block,block),0); cols=lax.broadcasted_iota(jnp.int32,(block,block),1)
        diag=jnp.where(rows<=cols,diag,-1e30)
        m=jnp.max(diag,axis=0,keepdims=True)
        if i:
            s=dot(k[:b],qs[:,b:n])
            m=jnp.maximum(m,jnp.max(s,axis=0,keepdims=True))
        p=jnp.exp(diag-m)
        l=jnp.sum(p,axis=0,keepdims=True)
        o=dot(vT[:,b:n],p.astype(BF))
        if i:
            p=jnp.exp(s-m)
            l=l+jnp.sum(p,axis=0,keepdims=True)
            o=o+dot(vT[:,:b],p.astype(BF))
        outs.append((o*(1.0/l)).astype(BF)); lses.append(m+jnp.log(l))
    return outs,lses

def onehot_rows(slot,first,count):
    ids=(lax.broadcasted_iota(jnp.int32,(count,slot.shape[1]),0)+first).astype(F32)
    return jnp.where(ids==slot,1.0,0.0).astype(BF)

def front_kernel(groups,cap,block,tok,rt,cot,g1,g2,wq,wk,wv,wo,
                 normed,q,k,v,att,lse,hid,pack,slot,cotarr,
                 cpack,n2,ssem,rsem,lsem):
    T,D=tok.shape
    R=256
    me=lax.axis_index("expert")
    barrier=pltpu.get_barrier_semaphore()
    def greet(i,c):
        pl.semaphore_signal(barrier,inc=1,device_id={"expert":xor(me,i,groups)},device_id_type=MESH)
        return c
    lax.fori_loop(1,groups,greet,0)
    routes=rt[...]
    e=jnp.where(lax.broadcasted_iota(jnp.int32,(groups,T),0)==routes,1.0,0.0)
    tri=jnp.where(lax.broadcasted_iota(jnp.int32,(T,T),0)<=lax.broadcasted_iota(jnp.int32,(T,T),1),1.0,0.0).astype(BF)
    cum=dot(e.astype(BF),tri)
    rank=jnp.sum(cum*e,axis=0,keepdims=True)-1.0
    slots=routes.astype(F32)*cap+rank
    slot[...]=slots
    pl.semaphore_wait(barrier,groups-1)
    def push(i,c):
        peer=xor(me,groups-1-i,groups)
        cpack[peer]=dot(onehot_rows(slots,peer*cap,cap),cot[...]).astype(BF)
        pltpu.make_async_remote_copy(src_ref=cpack.at[peer],dst_ref=cotarr.at[me],send_sem=ssem.at[peer],recv_sem=rsem.at[me],
            device_id={"expert":peer},device_id_type=MESH).start()
        return c
    lax.fori_loop(0,groups-1,push,0)
    cpack[me]=dot(onehot_rows(slots,me*cap,cap),cot[...]).astype(BF)
    own=pltpu.make_async_copy(cpack.at[me],cotarr.at[me],lsem)
    own.start()
    def norm_one(i,c):
        r=pl.ds(pl.multiple_of(i*R,R),R)
        u,_=norm_stats(tok[r,:].astype(F32))
        normed[r,:]=(u*g1[...]).astype(BF)
        return c
    lax.fori_loop(0,T//R,norm_one,0)
    def proj(i,c):
        s=pl.ds(pl.multiple_of(i*R,R),R)
        for w,o in ((wq,q),(wk,k),(wv,v)):
            o[s,:]=dg(w[:,s],normed[...],0,1).astype(BF)
        return c
    lax.fori_loop(0,D//R,proj,0)
    def head(h,c):
        s=pl.ds(pl.multiple_of(h*HEAD_DIM,HEAD_DIM),HEAD_DIM)
        outs,lses=fwd_head(q[s,:],k[s,:],v[s,:],block)
        att[s,:]=jnp.concatenate(outs,axis=1)
        lse[pl.ds(h,1),:]=jnp.concatenate(lses,axis=1)
        return c
    lax.fori_loop(0,D//HEAD_DIM,head,0)
    def out(i,c):
        r=pl.ds(pl.multiple_of(i*R,R),R)
        h=tok[r,:].astype(F32)+dg(att[:,r],wo[...],0,0)
        hid[r,:]=h
        u,_=norm_stats(h)
        n2[r,:]=(u*g2[...]).astype(BF)
        return c
    lax.fori_loop(0,T//R,out,0)
    def packing(i,c):
        pack[i]=dot(onehot_rows(slots,i*cap,cap),n2[...]).astype(BF)
        return c
    lax.fori_loop(0,groups,packing,0)
    own.wait()
    def finish(i,c):
        peer=xor(me,i,groups)
        pltpu.make_async_remote_copy(src_ref=cpack.at[peer],dst_ref=cotarr.at[peer],send_sem=ssem.at[peer],recv_sem=rsem.at[peer],
            device_id={"expert":peer},device_id_type=MESH).wait()
        return c
    lax.fori_loop(1,groups,finish,0)

def front(tokens,routes_row,cot,g1,g2,wq,wk,wv,wo,groups,cap,block=512):
    T,D=tokens.shape
    H=D//HEAD_DIM
    V=pl.BlockSpec(memory_space=pltpu.VMEM)
    A=pl.BlockSpec(memory_space=pl.ANY)
    sd=jax.ShapeDtypeStruct
    return pl.pallas_call(functools.partial(front_kernel,groups,cap,block),
      in_specs=[V]*9,out_specs=[V]*9+[A],
      out_shape=[sd((T,D),BF)]+[sd((D,T),BF)]*4+[sd((H,T),F32),sd((T,D),F32),sd((groups,cap,D),BF),sd((1,T),F32),sd((groups,cap,D),BF)],
      scratch_shapes=[pltpu.VMEM((groups,cap,D),BF),pltpu.VMEM((T,D),BF),pltpu.SemaphoreType.DMA((groups,)),pltpu.SemaphoreType.DMA((groups,)),pltpu.SemaphoreType.DMA],
      compiler_params=pltpu.CompilerParams(vmem_limit_bytes=60*2**20,collective_id=0,has_side_effects=True),
      name="front")(tokens,routes_row,cot,g1,g2,wq,wk,wv,wo)


F32=jnp.float32; BF=jnp.bfloat16
MESH=pl.DeviceIdType.MESH
def dot(a,b): return jnp.dot(a,b,preferred_element_type=F32)
def dg(a,b,ca,cb): return lax.dot_general(a,b,(((ca,),(cb,)),((),())),preferred_element_type=F32)
def xor(a,b,count):
    total=0; step=1
    while step<count:
        x=(a//step)%2; y=(b//step)%2
        total=total+step*(x+y-2*x*y); step*=2
    return total
SQ=math.sqrt(2/math.pi)
def gelu_pair(h):
    h2=h*h
    th=jnp.tanh(h*(SQ+SQ*0.044715*h2))
    half=0.5*(1.0+th)
    act=h*half
    slope=half+act*((1.0-th)*(SQ+3*SQ*0.044715*h2))
    return act,slope

def expert_kernel(groups,cap,early,pack,cotarr,up,down,gback,ret,chipu,chipd,xgot,act,
                  arr,upv,downv,cotv,gpre,actb,gst,retb,landu,landd,
                  psend,precv,gsend,grecv,wsem,retsem,actsem,tsem,ssend,srecv,xsend,xrecv,csem):
    rows=groups*cap
    D,F=upv.shape
    FT=1024
    me=lax.axis_index("expert")
    barrier=pltpu.get_barrier_semaphore()
    def greet(i,c):
        pl.semaphore_signal(barrier,inc=1,device_id={"expert":xor(me,i,groups)},device_id_type=MESH)
        return c
    lax.fori_loop(1,groups,greet,0)
    mine=lax.axis_index("replica")
    core=mine%2
    sibling=xor(mine,1,4); across=xor(mine,2,4)
    for peer in (sibling,across):
        pl.semaphore_signal(barrier,inc=1,device_id={"replica":peer},device_id_type=MESH)
    pl.semaphore_wait(barrier,groups+1)
    def at(j): return pl.ds(pl.multiple_of(j*cap,cap),cap)
    def dispatch(j,i):
        return pltpu.make_async_remote_copy(src_ref=pack.at[j],dst_ref=arr.at[at(me)],send_sem=psend.at[i],recv_sem=precv.at[i],
            device_id={"expert":j},device_id_type=MESH)
    def giveback(j,i):
        return pltpu.make_async_remote_copy(src_ref=gst.at[at(j)],dst_ref=gback.at[me],send_sem=gsend.at[i],recv_sem=grecv.at[i],
            device_id={"expert":j},device_id_type=MESH)
    half=groups//2
    def push(i,c):
        dispatch(xor(me,i,groups),i).start()
        return c
    lax.fori_loop(half,half+half//2,push,0)
    lax.fori_loop(1,half,push,0)
    own=pltpu.make_async_copy(pack.at[me],arr.at[at(me)],precv.at[0])
    own.start()
    cup=pltpu.make_async_copy(up,upv,wsem.at[0]); cup.start()
    ccot=pltpu.make_async_copy(cotarr,cotv,wsem.at[1]); ccot.start()
    cdown=pltpu.make_async_copy(down,downv,wsem.at[2]); cdown.start()
    cup.wait(); ccot.wait(); cdown.wait()
    def retcopy(j): return pltpu.make_async_copy(retb,ret.at[j],retsem)
    def actcopy(j): return pltpu.make_async_copy(actb,act.at[at(j)],actsem)
    def answer(i,c):
        giveback(xor(me,i,groups),i).start()
        return c
    def chunk(i,c):
        j=xor(me,i,groups)
        @pl.when(i==0)
        def _(): own.wait()
        @pl.when(i>0)
        def _(): dispatch(j,i).wait_recv()
        @pl.when(i==half-2)
        def _(): lax.fori_loop(half+half//2,groups,push,0)
        @pl.when(i==groups-1)
        def _():
            lax.fori_loop(half,groups-1,answer,0)
            lax.fori_loop(1,half,answer,0)
        @pl.when(i>=1)
        def _(): actcopy(j).wait()
        def tile(t,c):
            s=pl.ds(pl.multiple_of(t*FT,FT),FT)
            h=dot(arr[at(j),:],upv[:,s])
            g=dg(cotv[j],downv[s,:],1,1)
            a,slope=gelu_pair(h)
            actb[:,s]=a.astype(BF)
            gpre[at(j),s]=(g*slope).astype(BF)
            return c
        lax.fori_loop(0,F//FT,tile,0)
        gst[at(j),:]=dg(gpre[at(j),:],upv[...],1,1).astype(BF)
        @pl.when(i==groups-1)
        def _(): giveback(j,i).start()
        @pl.when(i==0)
        def _(): pltpu.make_async_copy(gst.at[at(j)],gback.at[me],grecv.at[0]).start()
        actcopy(j).start()
        @pl.when(i>=1)
        def _(): retcopy(j).wait()
        retb[...]=dot(actb[...],downv[...]).astype(BF)
        retcopy(j).start()
        return c
    lax.fori_loop(0,groups,chunk,0)
    retcopy(0).wait()
    actcopy(0).wait()
    def atile(t,b): return pltpu.make_async_copy(act.at[:,pl.ds(pl.multiple_of(t*D,D),D)],downv.at[pl.ds(b*rows,rows)],tsem.at[b])
    atile(0,0).start(); atile(1,1).start()
    S=512
    steps=F//(2*S)
    def shared(n):
        first=n*steps
        chip,land=(chipu,landu) if n==0 else (chipd,landd)
        def place(kind,b):
            if n==0:
                return upv.at[:,pl.ds((2*kind+b)*S,S)]
            return upv.at[pl.ds(b*S,S),pl.ds(kind*D,D)]
        def product(t,ref):
            if n==0:
                def part(k,c):
                    r=pl.ds(pl.multiple_of(k*S,S),S)
                    ref[r,:]=dg(arr[:,r],gpre[:,pl.ds(pl.multiple_of(t*S,S),S)],0,0).astype(BF)
                    return c
                lax.fori_loop(0,D//S,part,0)
            else:
                tb=(t//2)%2; Q=S//2
                def part(k,c):
                    a=downv[pl.ds(pl.multiple_of(tb*rows,rows),rows),pl.ds(pl.multiple_of((t%2)*S+k*Q,Q),Q)]
                    ref[pl.ds(pl.multiple_of(k*Q,Q),Q),:]=dg(a,cotv[...].reshape(rows,D),0,0).astype(BF)
                    return c
                lax.fori_loop(0,2,part,0)
        def tosib(s,b):
            return pltpu.make_async_remote_copy(src_ref=place(0,b),dst_ref=land.at[s],send_sem=ssend.at[first+s],recv_sem=srecv.at[first+s],
                device_id={"replica":sibling},device_id_type=MESH)
        def tochip(s,b): return pltpu.make_async_copy(place(1,b),chip.at[s],csem.at[first+s])
        def finish(s):
            tosib(s,s%2).wait_recv()
            ref=place(1,s%2)
            def add(k,c):
                r=pl.ds(pl.multiple_of(k*128,128),128)
                ref[r,:]=(ref[r,:].astype(F32)+land[s,r,:].astype(F32)).astype(BF)
                return c
            lax.fori_loop(0,ref.shape[0]//128,add,0)
            tochip(s,s%2).start()
        def leave(s):
            tochip(s,s%2).wait()
            if first+s<early: toacross(s).start()
        for s in range(steps):
            b=s%2
            if n==1: atile(s,b).wait()
            if s>=2: tosib(s-2,b).wait_send()
            product(2*s+1-core,place(0,b))
            tosib(s,b).start()
            if s>=1: finish(s-1)
            product(2*s+core,place(1,b))
            if n==1 and s+2<steps: atile(s+2,b).start()
            if s>=1: leave(s-1)
        finish(steps-1)
        for s in range(max(0,steps-2),steps): tosib(s,s%2).wait_send()
        leave(steps-1)
    def toacross(s):
        return pltpu.make_async_remote_copy(src_ref=chipu.at[s],dst_ref=xgot.at[s],send_sem=xsend.at[s],recv_sem=xrecv.at[s],
            device_id={"replica":across},device_id_type=MESH)
    shared(0)
    shared(1)
    pltpu.make_async_copy(gst.at[at(me)],gback.at[me],grecv.at[0]).wait()
    def finish(i,c):
        j=xor(me,i,groups)
        dispatch(j,i).wait_send()
        giveback(j,i).wait()
        return c
    lax.fori_loop(1,groups,finish,0)
    for s in range(early): toacross(s).wait()

def expert(pack,cotarr,up,down,early):
    groups,cap,D=pack.shape
    F=up.shape[1]; rows=groups*cap
    S=512; steps=F//(2*S)
    A=pl.BlockSpec(memory_space=pl.ANY)
    sd=jax.ShapeDtypeStruct
    DMA=pltpu.SemaphoreType.DMA
    su=sd((steps,D,S),BF); sdn=sd((steps,S,D),BF)
    return pl.pallas_call(functools.partial(expert_kernel,groups,cap,early),
      in_specs=[A]*4,out_specs=[A]*6,
      out_shape=[sd((groups,cap,D),BF)]*2+[su,sdn,sd((early,D,S),BF),sd((rows,F),BF)],
      scratch_shapes=[pltpu.VMEM((rows,D),BF),pltpu.VMEM((D,F),BF),pltpu.VMEM((F,D),BF),pltpu.VMEM((groups,cap,D),BF),pltpu.VMEM((rows,F),BF),
         pltpu.VMEM((cap,F),BF),pltpu.VMEM((rows,D),BF),pltpu.VMEM((cap,D),BF),pltpu.VMEM((steps,D,S),BF),pltpu.VMEM((steps,S,D),BF),
         DMA((groups,)),DMA((groups,)),DMA((groups,)),DMA((groups,)),DMA((3,)),DMA,DMA,DMA((2,)),
         DMA((2*steps,)),DMA((2*steps,)),DMA((early,)),DMA((early,)),DMA((2*steps,))],
      compiler_params=pltpu.CompilerParams(vmem_limit_bytes=63*2**20+2**19,collective_id=1,has_side_effects=True),
      name="experts")(pack,cotarr,up,down)


def bwd_head(qT,kT,vT,oT,doT,lse,block):
    seq=qT.shape[1]
    scale=HEAD_DIM**-0.5
    qs=qT*jnp.asarray(scale,BF)
    q=qs.T; k=kT.T; v=vT.T; do=doT.T
    delta=jnp.sum(oT.astype(F32)*doT.astype(F32),axis=0,keepdims=True)
    count=seq//block
    dqs=[None]*count; dks=[]; dvs=[]
    for j in range(count):
        b=j*block
        kj=k[b:b+block]; vj=v[b:b+block]
        s=dot(kj,qs[:,b:])
        n=seq-b
        rows=lax.broadcasted_iota(jnp.int32,(block,n),0); cols=lax.broadcasted_iota(jnp.int32,(block,n),1)
        p=jnp.where(rows<=cols,jnp.exp(s-lse[:,b:]),0.0)
        dp=dot(vj,doT[:,b:])
        ds=(p*(dp-delta[:,b:])).astype(BF)
        dvs.append(dot(p.astype(BF),do[b:]))
        dks.append(dot(ds,q[b:]))
        c=dot(kT[:,b:b+block],ds)
        for i in range(j,count):
            part=c[:,(i-j)*block:(i-j+1)*block]
            dqs[i]=part if dqs[i] is None else dqs[i]+part
    return [(x*scale).astype(BF).T for x in dqs],[x.astype(BF) for x in dks],[x.astype(BF) for x in dvs]

def back_kernel(groups,cap,block,early,
        gback,ret,slot,hid,cot,tok,normed,q,k,v,att,lse,g1,g2,wq,wk,wv,wo,chipu,chipd,xgot,
        output,gtok,dw,dgain,dup,ddown,rarr,xu,xd,
        vslots,vhid,vcot,vnormed,vq,vk,vv,vatt,vwo,ghl,datt,dq,dk,dv,vgt,dwv,rbuf,gbuf,
        isem,ssem,rsem,lsem,dsend,drecv,osem,xsend,xrecv,fsem,fout,fsend,frecv,gsend,grecv,credit):
    T,D=vnormed.shape
    R=256
    S=chipu.shape[2]
    steps=chipu.shape[0]
    parts=4
    W=D//parts
    rows=groups*cap
    me=lax.axis_index("expert")
    mine=lax.axis_index("replica")
    core=mine%2
    sibling=xor(mine,1,4); across=xor(mine,2,4)
    barrier=pltpu.get_barrier_semaphore()
    def greet(i,c):
        pl.semaphore_signal(barrier,inc=1,device_id={"expert":xor(me,i,groups)},device_id_type=MESH)
        return c
    lax.fori_loop(1,groups,greet,0)
    for peer in (sibling,across):
        pl.semaphore_signal(barrier,inc=1,device_id={"replica":peer},device_id_type=MESH)
    copies=[pltpu.make_async_copy(a,b,isem.at[i]) for i,(a,b) in enumerate(
        ((gback,vslots),(hid,vhid),(cot,vcot),(wo,vwo),(att,vatt),(q,vq),(k,vk),(v,vv),(normed,vnormed)))]
    for c in copies: c.start()
    pl.semaphore_wait(barrier,groups+1)
    def send(i):
        j=xor(me,i,groups)
        return pltpu.make_async_remote_copy(src_ref=ret.at[j],dst_ref=rarr.at[me],send_sem=ssem.at[i],recv_sem=rsem.at[i],
            device_id={"expert":j},device_id_type=MESH)
    def push(i,c):
        send(groups-i).start()
        return c
    lax.fori_loop(1,groups,push,0)
    own=pltpu.make_async_copy(ret.at[me],rarr.at[me],lsem); own.start()
    def toacross(n,s):
        src,dst=(chipu.at[s],xu.at[s-early]) if n==0 else (chipd.at[s],xd.at[s])
        return pltpu.make_async_remote_copy(src_ref=src,dst_ref=dst,send_sem=xsend.at[n,s],recv_sem=xrecv.at[n,s],
            device_id={"replica":across},device_id_type=MESH)
    late=[(0,s) for s in range(early,steps)]+[(1,s) for s in range(steps)]
    def spare(n,i):
        return vatt.at[:,pl.ds(i*S,S)] if n==0 else vnormed.at[pl.ds(i*S,S)]
    def finalize(n,s,got):
        a,b=spare(n,0),spare(n,1)
        l1=pltpu.make_async_copy((chipu if n==0 else chipd).at[s],a,fsem.at[0]); l1.start()
        l2=pltpu.make_async_copy(got,b,fsem.at[1]); l2.start()
        l1.wait(); l2.wait()
        def add(i,c):
            r=pl.ds(pl.multiple_of(i*128,128),128)
            a[r,:]=(a[r,:].astype(F32)+b[r,:].astype(F32)).astype(BF)
            return c
        lax.fori_loop(0,a.shape[0]//128,add,0)
        keep,share=leaving(n,s)
        keep.start(); share.start()
    def leaving(n,s):
        a=spare(n,0)
        d=pl.ds(pl.multiple_of((2*s+core)*S,S),S)
        there=dup.at[:,d] if n==0 else ddown.at[d]
        return (pltpu.make_async_copy(a,there,fout.at[n]),
            pltpu.make_async_remote_copy(src_ref=a,dst_ref=there,send_sem=fsend.at[n,s],recv_sem=frecv.at[n,s],
                device_id={"replica":sibling},device_id_type=MESH))
    def left(n,s):
        keep,share=leaving(n,s)
        keep.wait(); share.wait_send()
    for n,s in late[:2]: toacross(n,s).start()
    bits=[("replica",mine,1)]+[("expert",me,1<<b) for b in range(groups.bit_length()-1)]
    H=len(bits)
    base=[0]; other=[]; peers=[]
    for i,(axis,index,step) in enumerate(bits):
        n=D>>(i+1)
        bit=(index//step)%2
        other.append(base[-1]+(1-bit)*n)
        base.append(base[-1]+bit*n)
        peers.append({axis:index+step-2*step*bit})
    size=[D>>(i+1) for i in range(H)]+[D>>H]
    offset=[D-(D>>i) for i in range(H+1)]
    def piece(ref,c,first,n):
        return ref.at[:,pl.ds(pl.multiple_of(first,n),n),pl.ds(pl.multiple_of(c*W,W),W)]
    def move(c,k):
        if k<H:
            src=piece(dwv,c,other[k],size[k]); dst=piece(rbuf,c,offset[k],size[k]); peer=peers[k]
        elif k==H:
            src=piece(dwv,c,base[H],size[H]); dst=piece(rbuf,c,offset[H],size[H]); peer={"replica":across}
        else:
            i=2*H-k
            src=dst=piece(dwv,c,base[i+1],size[i]); peer=peers[i]
        return pltpu.make_async_remote_copy(src_ref=src,dst_ref=dst,send_sem=dsend.at[c,k],recv_sem=drecv.at[c,k],device_id=peer,device_id_type=MESH)
    def gather_in(c,k):
        first=base[min(k+1,H)]; n=size[k]
        m=min(n,64)
        cols=pl.ds(pl.multiple_of(c*W,W),W)
        def add(i,z):
            r=pl.ds(pl.multiple_of(first+i*m,m),m)
            o=pl.ds(pl.multiple_of(offset[k]+i*m,m),m)
            for x in range(4):
                dwv[x,r,cols]=(dwv[x,r,cols].astype(F32)+rbuf[x,o,cols].astype(F32)).astype(BF)
            return z
        lax.fori_loop(0,n//m,add,0)
    def out_dense(c):
        cols=pl.ds(pl.multiple_of(c*W,W),W)
        return pltpu.make_async_copy(dwv.at[:,:,cols],dw.at[:,:,cols],osem.at[c])
    K=2*H+2
    def progress(t):
        for k in range(K-1,-1,-1):
            c=t-k
            @pl.when((c>=0)&(c<parts))
            def _():
                if k>0:
                    move(c,k-1).wait()
                    if k<=H: pl.semaphore_signal(credit.at[c,k-1],inc=1,device_id=peers[k-1],device_id_type=MESH)
                if 0<k<=H+1: gather_in(c,k-1)
                if H<k<K-1: pl.semaphore_wait(credit.at[c,2*H-k],1)
                if k<K-1: move(c,k).start()
                else: out_dense(c).start()
    gbits=peers+[{"replica":across}]
    def gain_move(j):
        return pltpu.make_async_remote_copy(src_ref=dgain,dst_ref=gbuf.at[j],send_sem=gsend.at[j],recv_sem=grecv.at[j],device_id=gbits[j],device_id_type=MESH)
    def gain_step(j):
        if j>0:
            gain_move(j-1).wait()
            dgain[...]=dgain[...]+gbuf[j-1]
        if j<len(gbits): gain_move(j).start()
    def gathered(r):
        col=jnp.broadcast_to(slot[:,r],(128,R)).T[:,:1]
        ids=lax.broadcasted_iota(jnp.int32,(R,rows),1).astype(F32)
        return dot(jnp.where(ids==col,1.0,0.0).astype(BF),vslots[...].reshape(rows,D))
    for c in copies[:3]: c.wait()
    dgain[...]=jnp.zeros_like(dgain)
    def norm_two(i,c):
        r=pl.ds(pl.multiple_of(i*R,R),R)
        gs=gathered(r)
        u,inv=norm_stats(vhid[r,:])
        m=gs*g2[...]
        dgain[1:2,:]+=jnp.sum(gs*u,axis=0,keepdims=True)
        gh=vcot[r,:].astype(F32)+inv*(m-jnp.mean(m,axis=-1,keepdims=True)-u*jnp.mean(m*u,axis=-1,keepdims=True))
        vgt[r,:]=gh
        ghl[r,:]=gh.astype(BF)
        return c
    lax.fori_loop(0,T//R,norm_two,0)
    again=pltpu.make_async_copy(tok,vcot,isem.at[2]); again.start()
    for c in copies[3:5]: c.wait()
    def outproj(i,c):
        s=pl.ds(pl.multiple_of(i*R,R),R)
        datt[s,:]=dg(vwo[s,:],ghl[...],1,1).astype(BF)
        dwv[3,s,:]=dot(vatt[s,:],ghl[...]).astype(BF)
        return c
    lax.fori_loop(0,D//R,outproj,0)
    for c in copies[5:]: c.wait()
    w=2*HEAD_DIM
    def pair(h):
        col=pl.ds(pl.multiple_of(h*w,w),w)
        res=[]
        for a in range(2):
            s=pl.ds(pl.multiple_of(h*w+a*HEAD_DIM,HEAD_DIM),HEAD_DIM)
            res.append(bwd_head(vq[s,:],vk[s,:],vv[s,:],vatt[s,:],datt[s,:],lse[pl.ds(2*h+a,1),:],block))
        for ref,x,y in zip((dq,dk,dv),*res):
            for i in range(T//block):
                ref[i*block:(i+1)*block,col]=jnp.concatenate([x[i],y[i]],axis=1)
    loads=[pltpu.make_async_copy(a,b,isem.at[5+i]) for i,(a,b) in enumerate(((wq,vq),(wk,vk),(wv,vv)))]
    def time(t,c):
        @pl.when(t<parts)
        def _():
            per=D//w//parts
            def one(i,c):
                pair(t*per+i)
                return c
            lax.fori_loop(0,per,one,0)
            cols=pl.ds(pl.multiple_of(t*W,W),W)
            for n,x in enumerate((dq,dk,dv)):
                def rowpart(i,c):
                    s=pl.ds(pl.multiple_of(i*R,R),R)
                    dwv[n,s,cols]=dg(vnormed[:,s],x[:,cols],0,0).astype(BF)
                    return c
                lax.fori_loop(0,D//R,rowpart,0)
        @pl.when(t==parts-1)
        def _():
            for x in loads: x.start()
        @pl.when(t==parts)
        def _():
            again.wait()
            for x in loads: x.wait()
        @pl.when((t>=parts)&(t<2*parts))
        def _():
            n=T//parts
            r=pl.ds(pl.multiple_of((t-parts)*n,n),n)
            gn=dg(dq[r,:],vq[...],1,1)+dg(dk[r,:],vk[...],1,1)+dg(dv[r,:],vv[...],1,1)
            u,inv=norm_stats(vcot[r,:].astype(F32))
            m=gn*g1[...]
            dgain[0:1,:]+=jnp.sum(gn*u,axis=0,keepdims=True)
            vgt[r,:]+=inv*(m-jnp.mean(m,axis=-1,keepdims=True)-u*jnp.mean(m*u,axis=-1,keepdims=True))
        progress(t)
        for i,at in ((2,1),(4,4)):
            @pl.when(t==at)
            def _():
                for n,s in late[i:i+2]: toacross(n,s).start()
        @pl.when(t==2*parts)
        def _(): pltpu.make_async_copy(vgt,gtok,isem.at[0]).start()
        for j in range(ingain):
            @pl.when(t==2*parts+j)
            def _(): gain_step(j)
        for p,(n,s) in enumerate(order[:inloop]):
            @pl.when(t==parts+1+p)
            def _(): settle(p)
        return c
    order=[(0,s) for s in range(steps)]+[(1,s) for s in range(steps)]
    def settle(p):
        n,s=order[p]
        if p>0 and order[p-1][0]==n: left(n,s-1)
        if n==0 and s<early:
            finalize(n,s,xgot.at[s])
        else:
            toacross(n,s).wait()
            finalize(n,s,xu.at[s-early] if n==0 else xd.at[s])
        if p>0 and order[p-1][0]!=n: left(*order[p-1])
    last=parts+K-1
    inloop=steps+steps//2
    ingain=min(len(gbits)+1,last-2*parts)
    for n,s in late[6:]: toacross(n,s).start()
    lax.fori_loop(0,last,time,0)
    for j in range(ingain,len(gbits)+1): gain_step(j)
    own.wait()
    def finish(i,c):
        send(i).wait()
        return c
    lax.fori_loop(1,groups,finish,0)
    load=pltpu.make_async_copy(rarr,vslots,lsem); load.start()
    for p in range(inloop,len(order)): settle(p)
    load.wait()
    def final(i,c):
        r=pl.ds(pl.multiple_of(i*R,R),R)
        ghl[r,:]=(vhid[r,:]+gathered(r)).astype(BF)
        return c
    lax.fori_loop(0,T//R,final,0)
    last_out=pltpu.make_async_copy(ghl,output,isem.at[1]); last_out.start()
    left(*order[-1])
    for n,s in order: leaving(n,s)[1].wait_recv()
    for c in range(parts): out_dense(c).wait()
    pltpu.make_async_copy(vgt,gtok,isem.at[0]).wait()
    last_out.wait()

def back(gback,ret,slot,hid,cot,tok,normed,q,k,v,att,lse,g1,g2,wq,wk,wv,wo,chipu,chipd,xgot,block=256):
    groups,cap,D=ret.shape
    T=tok.shape[0]
    steps,_,S=chipu.shape
    early=xgot.shape[0]
    F=2*steps*S
    H=groups.bit_length()
    V=pl.BlockSpec(memory_space=pltpu.VMEM)
    A=pl.BlockSpec(memory_space=pl.ANY)
    sd=jax.ShapeDtypeStruct
    DMA=pltpu.SemaphoreType.DMA
    M=lambda *s: pltpu.VMEM(s,BF)
    return pl.pallas_call(functools.partial(back_kernel,groups,cap,block,early),
      in_specs=[A,A,V]+[A]*8+[V]*3+[A]*7,out_specs=[A]*3+[V]+[A]*5,
      out_shape=[sd((T,D),BF),sd((T,D),F32),sd((4,D,D),BF),sd((8,D),F32),sd((D,F),BF),sd((F,D),BF),sd((groups,cap,D),BF),
         sd((steps-early,D,S),BF),sd((steps,S,D),BF)],
      scratch_shapes=[M(groups,cap,D),pltpu.VMEM((T,D),F32),M(T,D),M(T,D),M(D,T),M(D,T),M(D,T),M(D,T),M(D,D),M(T,D),M(D,T),M(T,D),M(T,D),M(T,D),
         pltpu.VMEM((T,D),F32),M(4,D,D),M(4,D,D),pltpu.VMEM((H+1,8,D),F32),
         DMA((9,)),DMA((groups,)),DMA((groups,)),DMA,DMA((4,2*H+1)),DMA((4,2*H+1)),DMA((4,)),DMA((2,steps)),DMA((2,steps)),DMA((2,)),DMA((2,)),DMA((2,steps)),DMA((2,steps)),
         DMA((H+1,)),DMA((H+1,)),pltpu.SemaphoreType.REGULAR((4,H))],
      compiler_params=pltpu.CompilerParams(vmem_limit_bytes=63*2**20+2**19,collective_id=2,has_side_effects=True),
      name="back")(gback,ret,slot,hid,cot,tok,normed,q,k,v,att,lse,g1,g2,wq,wk,wv,wo,chipu,chipd,xgot)


def per_device(tokens,routes,gain_one,query_weight,key_weight,value_weight,out_weight,gain_two,up_weight,down_weight,cotangent):
    T,D=tokens.shape
    groups=lax.axis_size("expert")
    cap=2*T//groups
    g1=gain_one.reshape(1,D); g2=gain_two.reshape(1,D)
    weights=(query_weight,key_weight,value_weight,out_weight)
    normed,q,k,v,att,lse,hid,pack,slot,cotarr=front(tokens,routes.reshape(1,T),cotangent,g1,g2,*weights,groups,cap)
    gback,ret,chipu,chipd,xgot,_=expert(pack,cotarr,up_weight[0],down_weight[0],2)
    output,gtok,dw,dgain,dup,ddown,_,_,_=back(gback,ret,slot,hid,cotangent,tokens,normed,q,k,v,att,lse,g1,g2,*weights,chipu,chipd,xgot)
    ws=[dw[i].astype(F32) for i in range(4)]
    return (output,gtok,dgain[0],*ws,dgain[1],dup.astype(F32)[None],ddown.astype(F32)[None])
def solution(mesh):
    rows=P(("expert","replica"),None)
    each=P("expert",None,None)
    return jax.shard_map(per_device,mesh=mesh,
        in_specs=(rows,rows,P(),P(),P(),P(),P(),P(),each,each,rows),
        out_specs=(rows,rows,P(),P(),P(),P(),P(),P(),each,each),check_vma=False)
```

```python
import functools
import math

import jax
import jax.numpy as jnp
from jax import lax
from jax.experimental import pallas as pl
from jax.experimental.pallas import tpu as pltpu
from jax.sharding import PartitionSpec as P

HEAD_DIM=64
F32=jnp.float32; BF=jnp.bfloat16
MESH=pl.DeviceIdType.MESH
epsilon=1e-5
def dot(a,b): return jnp.dot(a,b,preferred_element_type=F32)
def dg(a,b,ca,cb): return lax.dot_general(a,b,(((ca,),(cb,)),((),())),preferred_element_type=F32)

def xor(a,b,count):
    total=0; step=1
    while step<count:
        x=(a//step)%2; y=(b//step)%2
        total=total+step*(x+y-2*x*y); step*=2
    return total

def norm_stats(rows):
    average=jnp.mean(rows,axis=-1,keepdims=True)
    centred=rows-average
    inverse=lax.rsqrt(jnp.mean(centred*centred,axis=-1,keepdims=True)+epsilon)
    return centred*inverse,inverse

def fwd_head(qT,kT,vT,block):
    seq=qT.shape[1]
    qs=qT*jnp.asarray(HEAD_DIM**-0.5,BF)
    k=kT.T
    outs=[]; lses=[]
    for i in range(seq//block):
        b=i*block; n=b+block
        diag=dot(k[b:n],qs[:,b:n])
        rows=lax.broadcasted_iota(jnp.int32,(block,block),0); cols=lax.broadcasted_iota(jnp.int32,(block,block),1)
        diag=jnp.where(rows<=cols,diag,-1e30)
        m=jnp.max(diag,axis=0,keepdims=True)
        if i:
            s=dot(k[:b],qs[:,b:n])
            m=jnp.maximum(m,jnp.max(s,axis=0,keepdims=True))
        p=jnp.exp(diag-m)
        l=jnp.sum(p,axis=0,keepdims=True)
        o=dot(vT[:,b:n],p.astype(BF))
        if i:
            p=jnp.exp(s-m)
            l=l+jnp.sum(p,axis=0,keepdims=True)
            o=o+dot(vT[:,:b],p.astype(BF))
        outs.append((o*(1.0/l)).astype(BF)); lses.append(m+jnp.log(l))
    return outs,lses

def onehot_rows(slot,first,count):
    ids=(lax.broadcasted_iota(jnp.int32,(count,slot.shape[1]),0)+first).astype(F32)
    return jnp.where(ids==slot,1.0,0.0).astype(BF)

def front_kernel(groups,cap,block,htok,rt,cot,g1,g2,hwq,hwk,hwv,hwo,
                 hnormed,hq,hk,hv,hatt,lse,hhid,hpack,slot,cotarr,
                 tok,wq,wk,wv,wo,normed,q,k,v,att,hid,pack,cpack,n2,ssem,rsem,lsem,isem,osem):
    loads=[pltpu.make_async_copy(a,b,isem.at[i]) for i,(a,b) in enumerate(((htok,tok),(hwq,wq),(hwk,wk),(hwv,wv),(hwo,wo)))]
    for c in loads: c.start()
    stores=[pltpu.make_async_copy(a,b,osem.at[i]) for i,(a,b) in enumerate(((normed,hnormed),(q,hq),(k,hk),(v,hv),(att,hatt),(hid,hhid),(pack,hpack)))]
    T,D=tok.shape
    R=256
    me=lax.axis_index("expert")
    barrier=pltpu.get_barrier_semaphore()
    def greet(i,c):
        pl.semaphore_signal(barrier,inc=1,device_id={"expert":xor(me,i,groups)},device_id_type=MESH)
        return c
    lax.fori_loop(1,groups,greet,0)
    routes=rt[...]
    e=jnp.where(lax.broadcasted_iota(jnp.int32,(groups,T),0)==routes,1.0,0.0)
    tri=jnp.where(lax.broadcasted_iota(jnp.int32,(T,T),0)<=lax.broadcasted_iota(jnp.int32,(T,T),1),1.0,0.0).astype(BF)
    cum=dot(e.astype(BF),tri)
    rank=jnp.sum(cum*e,axis=0,keepdims=True)-1.0
    slots=routes.astype(F32)*cap+rank
    slot[...]=slots
    pl.semaphore_wait(barrier,groups-1)
    def push(i,c):
        peer=xor(me,groups-1-i,groups)
        cpack[peer]=dot(onehot_rows(slots,peer*cap,cap),cot[...]).astype(BF)
        pltpu.make_async_remote_copy(src_ref=cpack.at[peer],dst_ref=cotarr.at[me],send_sem=ssem.at[peer],recv_sem=rsem.at[me],
            device_id={"expert":peer},device_id_type=MESH).start()
        return c
    lax.fori_loop(0,groups-1,push,0)
    cpack[me]=dot(onehot_rows(slots,me*cap,cap),cot[...]).astype(BF)
    own=pltpu.make_async_copy(cpack.at[me],cotarr.at[me],lsem)
    own.start()
    for c in loads: c.wait()
    def norm_one(i,c):
        r=pl.ds(pl.multiple_of(i*R,R),R)
        u,_=norm_stats(tok[r,:].astype(F32))
        normed[:,r]=(u*g1[...]).astype(BF).T
        return c
    lax.fori_loop(0,T//R,norm_one,0)
    stores[0].start()
    def proj(i,c):
        s=pl.ds(pl.multiple_of(i*R,R),R)
        for w,o in ((wq,q),(wk,k),(wv,v)):
            o[s,:]=dg(w[:,s],normed[...],0,0).astype(BF)
        return c
    lax.fori_loop(0,D//R,proj,0)
    for c in stores[1:4]: c.start()
    def head(h,c):
        s=pl.ds(pl.multiple_of(h*HEAD_DIM,HEAD_DIM),HEAD_DIM)
        outs,lses=fwd_head(q[s,:],k[s,:],v[s,:],block)
        att[s,:]=jnp.concatenate(outs,axis=1)
        lse[pl.ds(h,1),:]=jnp.concatenate(lses,axis=1)
        return c
    lax.fori_loop(0,D//HEAD_DIM,head,0)
    stores[4].start()
    def out(i,c):
        r=pl.ds(pl.multiple_of(i*R,R),R)
        h=tok[r,:].astype(F32)+dg(att[:,r],wo[...],0,0)
        hid[r,:]=h
        u,_=norm_stats(h)
        n2[r,:]=(u*g2[...]).astype(BF)
        return c
    lax.fori_loop(0,T//R,out,0)
    stores[5].start()
    def packing(i,c):
        pack[i]=dot(onehot_rows(slots,i*cap,cap),n2[...]).astype(BF)
        return c
    lax.fori_loop(0,groups,packing,0)
    stores[6].start()
    own.wait()
    for c in stores: c.wait()
    def finish(i,c):
        peer=xor(me,i,groups)
        pltpu.make_async_remote_copy(src_ref=cpack.at[peer],dst_ref=cotarr.at[peer],send_sem=ssem.at[peer],recv_sem=rsem.at[peer],
            device_id={"expert":peer},device_id_type=MESH).wait()
        return c
    lax.fori_loop(1,groups,finish,0)

def front(tokens,routes_row,cot,g1,g2,wq,wk,wv,wo,groups,cap,block=512):
    T,D=tokens.shape
    H=D//HEAD_DIM
    V=pl.BlockSpec(memory_space=pltpu.VMEM)
    A=pl.BlockSpec(memory_space=pl.ANY)
    sd=jax.ShapeDtypeStruct
    return pl.pallas_call(functools.partial(front_kernel,groups,cap,block),
      in_specs=[A]+[V]*4+[A]*4,out_specs=[A]*5+[V]+[A]*2+[V,A],
      out_shape=[sd((D,T),BF)]*5+[sd((H,T),F32),sd((T,D),F32),sd((groups,cap,D),BF),sd((1,T),F32),sd((groups,cap,D),BF)],
      scratch_shapes=[pltpu.VMEM((T,D),BF)]+[pltpu.VMEM((D,D),BF)]*4+[pltpu.VMEM((D,T),BF)]*5+[pltpu.VMEM((T,D),F32),pltpu.VMEM((groups,cap,D),BF),pltpu.VMEM((groups,cap,D),BF),pltpu.VMEM((T,D),BF),pltpu.SemaphoreType.DMA((groups,)),pltpu.SemaphoreType.DMA((groups,)),pltpu.SemaphoreType.DMA,pltpu.SemaphoreType.DMA((5,)),pltpu.SemaphoreType.DMA((7,))],
      compiler_params=pltpu.CompilerParams(vmem_limit_bytes=60*2**20,collective_id=0,has_side_effects=True),
      name="front")(tokens,routes_row,cot,g1,g2,wq,wk,wv,wo)


F32=jnp.float32; BF=jnp.bfloat16
MESH=pl.DeviceIdType.MESH
def dot(a,b): return jnp.dot(a,b,preferred_element_type=F32)
def dg(a,b,ca,cb): return lax.dot_general(a,b,(((ca,),(cb,)),((),())),preferred_element_type=F32)
def xor(a,b,count):
    total=0; step=1
    while step<count:
        x=(a//step)%2; y=(b//step)%2
        total=total+step*(x+y-2*x*y); step*=2
    return total
SQ=math.sqrt(2/math.pi)
def gelu_pair(h):
    h2=h*h
    th=jnp.tanh(h*(SQ+SQ*0.044715*h2))
    half=0.5*(1.0+th)
    act=h*half
    slope=half+act*((1.0-th)*(SQ+3*SQ*0.044715*h2))
    return act,slope

def expert_kernel(groups,cap,early,pack,cotarr,up,down,gback,ret,chipu,chipd,xgot,act,
                  arr,upv,downv,cotv,gpre,actb,gst,retb,landu,landd,
                  psend,precv,gsend,grecv,wsem,retsem,actsem,tsem,ssend,srecv,xsend,xrecv,csem):
    rows=groups*cap
    D,F=upv.shape
    FT=1024
    me=lax.axis_index("expert")
    barrier=pltpu.get_barrier_semaphore()
    def greet(i,c):
        pl.semaphore_signal(barrier,inc=1,device_id={"expert":xor(me,i,groups)},device_id_type=MESH)
        return c
    lax.fori_loop(1,groups,greet,0)
    mine=lax.axis_index("replica")
    core=mine%2
    sibling=xor(mine,1,4); across=xor(mine,2,4)
    for peer in (sibling,across):
        pl.semaphore_signal(barrier,inc=1,device_id={"replica":peer},device_id_type=MESH)
    pl.semaphore_wait(barrier,groups+1)
    def at(j): return pl.ds(pl.multiple_of(j*cap,cap),cap)
    def dispatch(j,i):
        return pltpu.make_async_remote_copy(src_ref=pack.at[j],dst_ref=arr.at[at(me)],send_sem=psend.at[i],recv_sem=precv.at[i],
            device_id={"expert":j},device_id_type=MESH)
    def giveback(j,i):
        return pltpu.make_async_remote_copy(src_ref=gst.at[at(j)],dst_ref=gback.at[me],send_sem=gsend.at[i],recv_sem=grecv.at[i],
            device_id={"expert":j},device_id_type=MESH)
    half=groups//2
    def code(i): return i+(i//half)*((i+half//2)%half+half-i)
    def push(i,c):
        dispatch(xor(me,code(i),groups),i).start()
        return c
    lax.fori_loop(half,half+half//2,push,0)
    lax.fori_loop(1,half,push,0)
    own=pltpu.make_async_copy(pack.at[me],arr.at[at(me)],precv.at[0])
    own.start()
    cup=pltpu.make_async_copy(up,upv,wsem.at[0]); cup.start()
    ccot=pltpu.make_async_copy(cotarr,cotv,wsem.at[1]); ccot.start()
    cdown=pltpu.make_async_copy(down,downv,wsem.at[2]); cdown.start()
    cup.wait(); ccot.wait(); cdown.wait()
    def retcopy(j): return pltpu.make_async_copy(retb,ret.at[j],retsem)
    def actcopy(j): return pltpu.make_async_copy(actb,act.at[at(j)],actsem)
    def results(j):
        retb[...]=dot(actb[...],downv[...]).astype(BF)
        retcopy(j).start()
    def answer(i,c):
        giveback(xor(me,code(i),groups),i).start()
        return c
    def chunk(i,c):
        j=xor(me,code(i),groups)
        @pl.when(i==0)
        def _(): own.wait()
        @pl.when(i>0)
        def _(): dispatch(j,i).wait_recv()
        @pl.when(i==half-2)
        def _(): lax.fori_loop(half+half//2,groups,push,0)
        @pl.when(i==groups-1)
        def _():
            lax.fori_loop(half,groups-1,answer,0)
            lax.fori_loop(1,half,answer,0)
        @pl.when(i>=1)
        def _(): actcopy(j).wait()
        def tile(t,c):
            s=pl.ds(pl.multiple_of(t*FT,FT),FT)
            h=dot(arr[at(j),:],upv[:,s])
            g=dg(cotv[j],downv[s,:],1,1)
            a,slope=gelu_pair(h)
            actb[:,s]=a.astype(BF)
            gpre[at(j),s]=(g*slope).astype(BF)
            return c
        lax.fori_loop(0,F//FT,tile,0)
        gst[at(j),:]=dg(gpre[at(j),:],upv[...],1,1).astype(BF)
        @pl.when(i==groups-1)
        def _(): giveback(j,i).start()
        @pl.when(i==0)
        def _(): pltpu.make_async_copy(gst.at[at(j)],gback.at[me],grecv.at[0]).start()
        actcopy(j).start()
        @pl.when((i>=1)&(i<groups-1))
        def _(): retcopy(j).wait()
        @pl.when(i<groups-1)
        def _(): results(j)
        return c
    lax.fori_loop(0,groups,chunk,0)
    actcopy(0).wait()
    def atile(t,b): return pltpu.make_async_copy(act.at[:,pl.ds(pl.multiple_of(t*D,D),D)],downv.at[pl.ds(b*rows,rows)],tsem.at[b])
    S=512
    steps=F//(2*S)
    def shared(n):
        first=n*steps
        chip,land=(chipu,landu) if n==0 else (chipd,landd)
        def place(kind,b):
            if n==0:
                return upv.at[:,pl.ds((2*kind+b)*S,S)]
            return upv.at[pl.ds(b*S,S),pl.ds(kind*D,D)]
        def product(t,ref):
            if n==0:
                def part(k,c):
                    r=pl.ds(pl.multiple_of(k*S,S),S)
                    ref[r,:]=dg(arr[:,r],gpre[:,pl.ds(pl.multiple_of(t*S,S),S)],0,0).astype(BF)
                    return c
                lax.fori_loop(0,D//S,part,0)
            else:
                tb=(t//2)%2; Q=S//2
                def part(k,c):
                    a=downv[pl.ds(pl.multiple_of(tb*rows,rows),rows),pl.ds(pl.multiple_of((t%2)*S+k*Q,Q),Q)]
                    ref[pl.ds(pl.multiple_of(k*Q,Q),Q),:]=dg(a,cotv[...].reshape(rows,D),0,0).astype(BF)
                    return c
                lax.fori_loop(0,2,part,0)
        def tosib(s,b):
            return pltpu.make_async_remote_copy(src_ref=place(0,b),dst_ref=land.at[s],send_sem=ssend.at[first+s],recv_sem=srecv.at[first+s],
                device_id={"replica":sibling},device_id_type=MESH)
        def tochip(s,b): return pltpu.make_async_copy(place(1,b),chip.at[s],csem.at[first+s])
        def finish(s):
            tosib(s,s%2).wait_recv()
            ref=place(1,s%2)
            def add(k,c):
                r=pl.ds(pl.multiple_of(k*128,128),128)
                ref[r,:]=(ref[r,:].astype(F32)+land[s,r,:].astype(F32)).astype(BF)
                return c
            lax.fori_loop(0,ref.shape[0]//128,add,0)
            tochip(s,s%2).start()
        def leave(s):
            tochip(s,s%2).wait()
            if first+s<early: toacross(s).start()
        for s in range(steps):
            b=s%2
            if n==1: atile(s,b).wait()
            if s>=2: tosib(s-2,b).wait_send()
            product(2*s+1-core,place(0,b))
            tosib(s,b).start()
            if s>=2: finish(s-1)
            product(2*s+core,place(1,b))
            if n==1 and s+2<steps: atile(s+2,b).start()
            if s==0: finish(0)
            if s!=1: leave(max(s-1,0))
        finish(steps-1)
        for s in range(max(0,steps-2),steps): tosib(s,s%2).wait_send()
        leave(steps-1)
    def toacross(s):
        return pltpu.make_async_remote_copy(src_ref=chipu.at[s],dst_ref=xgot.at[s],send_sem=xsend.at[s],recv_sem=xrecv.at[s],
            device_id={"replica":across},device_id_type=MESH)
    shared(0)
    retcopy(0).wait()
    results(xor(me,code(groups-1),groups))
    retcopy(0).wait()
    atile(0,0).start(); atile(1,1).start()
    shared(1)
    pltpu.make_async_copy(gst.at[at(me)],gback.at[me],grecv.at[0]).wait()
    def finish(i,c):
        j=xor(me,code(i),groups)
        dispatch(j,i).wait_send()
        giveback(j,i).wait()
        return c
    lax.fori_loop(1,groups,finish,0)
    for s in range(early): toacross(s).wait()

def expert(pack,cotarr,up,down,early):
    groups,cap,D=pack.shape
    F=up.shape[1]; rows=groups*cap
    S=512; steps=F//(2*S)
    A=pl.BlockSpec(memory_space=pl.ANY)
    sd=jax.ShapeDtypeStruct
    DMA=pltpu.SemaphoreType.DMA
    su=sd((steps,D,S),BF); sdn=sd((steps,S,D),BF)
    return pl.pallas_call(functools.partial(expert_kernel,groups,cap,early),
      in_specs=[A]*4,out_specs=[A]*6,
      out_shape=[sd((groups,cap,D),BF)]*2+[su,sdn,sd((early,D,S),BF),sd((rows,F),BF)],
      scratch_shapes=[pltpu.VMEM((rows,D),BF),pltpu.VMEM((D,F),BF),pltpu.VMEM((F,D),BF),pltpu.VMEM((groups,cap,D),BF),pltpu.VMEM((rows,F),BF),
         pltpu.VMEM((cap,F),BF),pltpu.VMEM((rows,D),BF),pltpu.VMEM((cap,D),BF),pltpu.VMEM((steps,D,S),BF),pltpu.VMEM((steps,S,D),BF),
         DMA((groups,)),DMA((groups,)),DMA((groups,)),DMA((groups,)),DMA((3,)),DMA,DMA,DMA((2,)),
         DMA((2*steps,)),DMA((2*steps,)),DMA((early,)),DMA((early,)),DMA((2*steps,))],
      compiler_params=pltpu.CompilerParams(vmem_limit_bytes=63*2**20+2**19,collective_id=1,has_side_effects=True),
      name="experts")(pack,cotarr,up,down)


def bwd_head(qT,kT,vT,oT,doT,lse,block):
    seq=qT.shape[1]
    scale=HEAD_DIM**-0.5
    qs=qT*jnp.asarray(scale,BF)
    q=qs.T; k=kT.T; v=vT.T; do=doT.T
    delta=jnp.sum(oT.astype(F32)*doT.astype(F32),axis=0,keepdims=True)
    count=seq//block
    dqs=[None]*count; dks=[]; dvs=[]
    for j in range(count):
        b=j*block
        kj=k[b:b+block]; vj=v[b:b+block]
        s=dot(kj,qs[:,b:])
        n=seq-b
        rows=lax.broadcasted_iota(jnp.int32,(block,n),0); cols=lax.broadcasted_iota(jnp.int32,(block,n),1)
        p=jnp.where(rows<=cols,jnp.exp(s-lse[:,b:]),0.0)
        dp=dot(vj,doT[:,b:])
        ds=(p*(dp-delta[:,b:])).astype(BF)
        dvs.append(dot(p.astype(BF),do[b:]))
        dks.append(dot(ds,q[b:]))
        c=dot(kT[:,b:b+block],ds)
        for i in range(j,count):
            part=c[:,(i-j)*block:(i-j+1)*block]
            dqs[i]=part if dqs[i] is None else dqs[i]+part
    return [(x*scale).astype(BF).T for x in dqs],[x.astype(BF) for x in dks],[x.astype(BF) for x in dvs]

def back_kernel(groups,cap,block,early,tile_at,ret_at,
        gback,ret,slot,hid,cot,tok,normed,q,k,v,att,lse,g1,g2,wq,wk,wv,wo,chipu,chipd,xgot,
        output,gtok,dw,dgain,dup,ddown,rarr,xu,xd,
        vslots,vhid,vcot,vnormed,vq,vk,vv,vatt,vwo,ghl,datt,dq,dk,dv,vgt,dwv,rbuf,gbuf,
        isem,ssem,rsem,lsem,dsend,drecv,osem,xsend,xrecv,fsem,fout,fsend,frecv,gsend,grecv,credit):
    D,T=vnormed.shape
    R=256
    S=chipu.shape[2]
    steps=chipu.shape[0]
    parts=4
    W=D//parts
    rows=groups*cap
    me=lax.axis_index("expert")
    mine=lax.axis_index("replica")
    core=mine%2
    sibling=xor(mine,1,4); across=xor(mine,2,4)
    barrier=pltpu.get_barrier_semaphore()
    def greet(i,c):
        pl.semaphore_signal(barrier,inc=1,device_id={"expert":xor(me,i,groups)},device_id_type=MESH)
        return c
    lax.fori_loop(1,groups,greet,0)
    for peer in (sibling,across):
        pl.semaphore_signal(barrier,inc=1,device_id={"replica":peer},device_id_type=MESH)
    copies=[pltpu.make_async_copy(a,b,isem.at[i]) for i,(a,b) in enumerate(
        ((gback,vslots),(hid,vhid),(cot,vcot),(wo,vwo),(att,vatt),(q,vq),(k,vk),(v,vv),(normed,vnormed)))]
    for c in copies: c.start()
    pl.semaphore_wait(barrier,groups+1)
    def send(i):
        j=xor(me,i,groups)
        return pltpu.make_async_remote_copy(src_ref=ret.at[j],dst_ref=rarr.at[me],send_sem=ssem.at[i],recv_sem=rsem.at[i],
            device_id={"expert":j},device_id_type=MESH)
    def push(i,c):
        send(i).start()
        return c
    def push_share(p):
        lax.fori_loop(1+p*(groups-1)//7,1+(p+1)*(groups-1)//7,push,0)
    for p in range(7):
        if ret_at[p]<0: push_share(p)
    own=pltpu.make_async_copy(ret.at[me],rarr.at[me],lsem); own.start()
    def toacross(n,s,p):
        src,dst=(chipu.at[s],xu.at[s-early]) if n==0 else (chipd.at[s],xd.at[s])
        m=src.shape[0]//2
        return pltpu.make_async_remote_copy(src_ref=src.at[pl.ds(p*m,m)],dst_ref=dst.at[pl.ds(p*m,m)],send_sem=xsend.at[n,2*s+p],recv_sem=xrecv.at[n,2*s+p],
            device_id={"replica":across},device_id_type=MESH)
    late=[(n,s,p) for n in range(2) for s in range(0 if n else early,steps) for p in range(2)]
    def spare(n,i):
        return vatt.at[:,pl.ds(i*S,S)] if n==0 else vnormed.at[pl.ds(i*S,S)]
    def finalize(n,s,got):
        a,b=spare(n,0),spare(n,1)
        l1=pltpu.make_async_copy((chipu if n==0 else chipd).at[s],a,fsem.at[0]); l1.start()
        l2=pltpu.make_async_copy(got,b,fsem.at[1]); l2.start()
        l1.wait(); l2.wait()
        def add(i,c):
            r=pl.ds(pl.multiple_of(i*128,128),128)
            a[r,:]=(a[r,:].astype(F32)+b[r,:].astype(F32)).astype(BF)
            return c
        lax.fori_loop(0,a.shape[0]//128,add,0)
        keep,share=leaving(n,s)
        keep.start(); share.start()
    def leaving(n,s):
        a=spare(n,0)
        d=pl.ds(pl.multiple_of((2*s+core)*S,S),S)
        there=dup.at[:,d] if n==0 else ddown.at[d]
        return (pltpu.make_async_copy(a,there,fout.at[n]),
            pltpu.make_async_remote_copy(src_ref=a,dst_ref=there,send_sem=fsend.at[n,s],recv_sem=frecv.at[n,s],
                device_id={"replica":sibling},device_id_type=MESH))
    def left(n,s):
        keep,share=leaving(n,s)
        keep.wait(); share.wait_send()
    for i,x in enumerate(late):
        if tile_at[i]<0: toacross(*x).start()
    V=W//2
    half=[(1<<b) for b in range(groups.bit_length()-1)]
    def partner(index,step): return index+step-2*step*((index//step)%2)
    paths=[]
    for steps_of in (half[:-1],half[1::-1]+half[2:-1] if len(half)>2 else half[:-1]):
        base=[0]; other=[]; peers=[]
        for i,(axis,index,step) in enumerate([("replica",mine,1)]+[("expert",me,b) for b in steps_of]):
            n=D>>(i+1)
            bit=(index//step)%2
            other.append(base[-1]+(1-bit)*n)
            base.append(base[-1]+bit*n)
            peers.append({axis:partner(index,step)})
        paths.append((base,other,peers))
    whole=[{"expert":partner(me,half[-1])},{"replica":across}]
    H=len(paths[0][2])
    size=[D>>(i+1) for i in range(H)]+[D>>H]*2
    offset=[D-(D>>i) for i in range(H+1)]+[D]
    def columns(c,h): return pl.ds(pl.multiple_of(c*W+h*V,V),V)
    def piece(ref,c,h,first,n):
        return ref.at[:,pl.ds(pl.multiple_of(first,n),n),columns(c,h)]
    def move(c,h,k):
        base,other,peers=paths[h]
        if k<H:
            src=piece(dwv,c,h,other[k],size[k]); dst=piece(rbuf,c,h,offset[k],size[k]); peer=peers[k]
        elif k<H+2:
            src=piece(dwv,c,h,base[H],size[k]); dst=piece(rbuf,c,h,offset[k],size[k]); peer=whole[k-H]
        else:
            i=2*H+1-k
            src=dst=piece(dwv,c,h,base[i+1],size[i]); peer=peers[i]
        return pltpu.make_async_remote_copy(src_ref=src,dst_ref=dst,send_sem=dsend.at[2*c+h,k],recv_sem=drecv.at[2*c+h,k],device_id=peer,device_id_type=MESH)
    def gather_in(c,h,k):
        first=paths[h][0][min(k+1,H)]; n=size[k]
        m=min(n,64)
        cols=columns(c,h)
        def add(i,z):
            r=pl.ds(pl.multiple_of(first+i*m,m),m)
            o=pl.ds(pl.multiple_of(offset[k]+i*m,m),m)
            for x in range(4):
                dwv[x,r,cols]=(dwv[x,r,cols].astype(F32)+rbuf[x,o,cols].astype(F32)).astype(BF)
            return z
        lax.fori_loop(0,n//m,add,0)
    def out_dense(c):
        cols=pl.ds(pl.multiple_of(c*W,W),W)
        return pltpu.make_async_copy(dwv.at[:,:,cols],dw.at[:,:,cols],osem.at[c])
    K=2*H+3
    last=parts+K-1
    def progress(t):
        for k in [x for x in range(K-1,-1,-1) if x!=H+2]+[H+2]:
            c=t-k
            @pl.when((c>=0)&(c<parts))
            def _():
                for h in range(2):
                    if k>0:
                        move(c,h,k-1).wait()
                        if k<=H: pl.semaphore_signal(credit.at[2*c+h,k-1],inc=1,device_id=paths[h][2][k-1],device_id_type=MESH)
                    if 0<k<=H+2: gather_in(c,h,k-1)
                    if H+2<=k<K-1: pl.semaphore_wait(credit.at[2*c+h,2*H+1-k],1)
                    if k<K-1: move(c,h,k).start()
                if k==K-1: out_dense(c).start()
    gbits=paths[0][2]+whole
    def gain_move(j):
        return pltpu.make_async_remote_copy(src_ref=dgain,dst_ref=gbuf.at[j],send_sem=gsend.at[j],recv_sem=grecv.at[j],device_id=gbits[j],device_id_type=MESH)
    def gain_step(j):
        if j>0:
            gain_move(j-1).wait()
            dgain[...]=dgain[...]+gbuf[j-1]
        if j<len(gbits): gain_move(j).start()
    def gathered(r):
        col=jnp.broadcast_to(slot[:,r],(128,R)).T[:,:1]
        ids=lax.broadcasted_iota(jnp.int32,(R,rows),1).astype(F32)
        return dot(jnp.where(ids==col,1.0,0.0).astype(BF),vslots[...].reshape(rows,D))
    for c in copies[:3]: c.wait()
    dgain[...]=jnp.zeros_like(dgain)
    def norm_two(i,c):
        r=pl.ds(pl.multiple_of(i*R,R),R)
        gs=gathered(r)
        u,inv=norm_stats(vhid[r,:])
        m=gs*g2[...]
        dgain[1:2,:]+=jnp.sum(gs*u,axis=0,keepdims=True)
        gh=vcot[r,:].astype(F32)+inv*(m-jnp.mean(m,axis=-1,keepdims=True)-u*jnp.mean(m*u,axis=-1,keepdims=True))
        vgt[r,:]=gh
        ghl[r,:]=gh.astype(BF)
        return c
    lax.fori_loop(0,T//R,norm_two,0)
    again=pltpu.make_async_copy(tok,vcot,isem.at[2]); again.start()
    for c in copies[3:5]: c.wait()
    def outproj(i,c):
        s=pl.ds(pl.multiple_of(i*R,R),R)
        datt[s,:]=dg(vwo[s,:],ghl[...],1,1).astype(BF)
        dwv[3,s,:]=dot(vatt[s,:],ghl[...]).astype(BF)
        return c
    lax.fori_loop(0,D//R,outproj,0)
    for c in copies[5:]: c.wait()
    w=2*HEAD_DIM
    def pair(h):
        col=pl.ds(pl.multiple_of(h*w,w),w)
        res=[]
        for a in range(2):
            s=pl.ds(pl.multiple_of(h*w+a*HEAD_DIM,HEAD_DIM),HEAD_DIM)
            res.append(bwd_head(vq[s,:],vk[s,:],vv[s,:],vatt[s,:],datt[s,:],lse[pl.ds(2*h+a,1),:],block))
        for ref,x,y in zip((dq,dk,dv),*res):
            for i in range(T//block):
                ref[i*block:(i+1)*block,col]=jnp.concatenate([x[i],y[i]],axis=1)
    loads=[pltpu.make_async_copy(a,b,isem.at[5+i]) for i,(a,b) in enumerate(((wq,vq),(wk,vk),(wv,vv)))]
    def time(t,c):
        @pl.when(t<parts)
        def _():
            per=D//w//parts
            def one(i,c):
                pair(t*per+i)
                return c
            lax.fori_loop(0,per,one,0)
            cols=pl.ds(pl.multiple_of(t*W,W),W)
            for n,x in enumerate((dq,dk,dv)):
                def rowpart(i,c):
                    s=pl.ds(pl.multiple_of(i*2*R,2*R),2*R)
                    dwv[n,s,cols]=dot(vnormed[s,:],x[:,cols]).astype(BF)
                    return c
                lax.fori_loop(0,D//(2*R),rowpart,0)
        @pl.when(t==parts-1)
        def _():
            for x in loads: x.start()
        @pl.when(t==parts)
        def _():
            again.wait()
            for x in loads: x.wait()
        @pl.when((t>=parts)&(t<2*parts))
        def _():
            n=T//parts
            r=pl.ds(pl.multiple_of((t-parts)*n,n),n)
            gn=dg(dq[r,:],vq[...],1,1)+dg(dk[r,:],vk[...],1,1)+dg(dv[r,:],vv[...],1,1)
            u,inv=norm_stats(vcot[r,:].astype(F32))
            m=gn*g1[...]
            dgain[0:1,:]+=jnp.sum(gn*u,axis=0,keepdims=True)
            vgt[r,:]+=inv*(m-jnp.mean(m,axis=-1,keepdims=True)-u*jnp.mean(m*u,axis=-1,keepdims=True))
        progress(t)
        for at in range(last):
            if at in tile_at or at in ret_at:
                @pl.when(t==at)
                def _():
                    for i,x in enumerate(late):
                        if tile_at[i]==at: toacross(*x).start()
                    for p in range(7):
                        if ret_at[p]==at: push_share(p)
        @pl.when(t==2*parts)
        def _(): pltpu.make_async_copy(vgt,gtok,isem.at[0]).start()
        @pl.when(t==2*parts)
        def _(): returned()
        @pl.when((t>=2*parts)&(t<3*parts))
        def _(): final(t-2*parts)
        for j in range(ingain):
            @pl.when(t==2*parts+j)
            def _(): gain_step(j)
        for p,(n,s) in enumerate(order[:inloop]):
            @pl.when(t==parts+1+p)
            def _(): settle(p)
        return c
    def returned():
        own.wait()
        def finish(i,c):
            send(i).wait()
            return c
        lax.fori_loop(1,groups,finish,0)
        load=pltpu.make_async_copy(rarr,vslots,lsem); load.start(); load.wait()
    def final(i):
        n=T//parts
        r=pl.ds(pl.multiple_of(i*n,n),n)
        ghl[r,:]=(vhid[r,:]+gathered(r)).astype(BF)
    order=[(0,s) for s in range(steps)]+[(1,s) for s in range(steps)]
    def settle(p):
        n,s=order[p]
        if p>0 and order[p-1][0]==n: left(n,s-1)
        if n==0 and s<early:
            finalize(n,s,xgot.at[s])
        else:
            for i in range(2): toacross(n,s,i).wait()
            finalize(n,s,xu.at[s-early] if n==0 else xd.at[s])
        if p>0 and order[p-1][0]!=n: left(*order[p-1])
    inloop=steps+steps//2
    ingain=min(len(gbits)+1,last-2*parts)
    lax.fori_loop(0,last,time,0)
    for j in range(ingain,len(gbits)+1): gain_step(j)
    for p in range(inloop,len(order)): settle(p)
    last_out=pltpu.make_async_copy(ghl,output,isem.at[1]); last_out.start()
    left(*order[-1])
    for n,s in order: leaving(n,s)[1].wait_recv()
    for c in range(parts): out_dense(c).wait()
    pltpu.make_async_copy(vgt,gtok,isem.at[0]).wait()
    last_out.wait()

def back(gback,ret,slot,hid,cot,tok,normed,q,k,v,att,lse,g1,g2,wq,wk,wv,wo,chipu,chipd,xgot,tile_at,ret_at,block=256):
    groups,cap,D=ret.shape
    T=tok.shape[0]
    steps,_,S=chipu.shape
    early=xgot.shape[0]
    F=2*steps*S
    H=groups.bit_length()-1
    V=pl.BlockSpec(memory_space=pltpu.VMEM)
    A=pl.BlockSpec(memory_space=pl.ANY)
    sd=jax.ShapeDtypeStruct
    DMA=pltpu.SemaphoreType.DMA
    M=lambda *s: pltpu.VMEM(s,BF)
    return pl.pallas_call(functools.partial(back_kernel,groups,cap,block,early,tile_at,ret_at),
      in_specs=[A,A,V]+[A]*8+[V]*3+[A]*7,out_specs=[A]*3+[V]+[A]*5,
      out_shape=[sd((T,D),BF),sd((T,D),F32),sd((4,D,D),BF),sd((8,D),F32),sd((D,F),BF),sd((F,D),BF),sd((groups,cap,D),BF),
         sd((steps-early,D,S),BF),sd((steps,S,D),BF)],
      scratch_shapes=[M(groups,cap,D),pltpu.VMEM((T,D),F32),M(T,D),M(D,T),M(D,T),M(D,T),M(D,T),M(D,T),M(D,D),M(T,D),M(D,T),M(T,D),M(T,D),M(T,D),
         pltpu.VMEM((T,D),F32),M(4,D,D),M(4,D+(D>>H),D),pltpu.VMEM((H+2,8,D),F32),
         DMA((9,)),DMA((groups,)),DMA((groups,)),DMA,DMA((8,2*H+2)),DMA((8,2*H+2)),DMA((4,)),DMA((2,2*steps)),DMA((2,2*steps)),DMA((2,)),DMA((2,)),DMA((2,steps)),DMA((2,steps)),
         DMA((H+2,)),DMA((H+2,)),pltpu.SemaphoreType.REGULAR((8,H))],
      compiler_params=pltpu.CompilerParams(vmem_limit_bytes=63*2**20+2**19,collective_id=2,has_side_effects=True),
      name="back")(gback,ret,slot,hid,cot,tok,normed,q,k,v,att,lse,g1,g2,wq,wk,wv,wo,chipu,chipd,xgot)


def widen_kernel(dup,ddown,dw,output,gtok,gup,gdown,*rest):
    gup[...]=dup[...].astype(F32)
    gdown[...]=ddown[...].astype(F32)
    for i in range(4): rest[i][...]=dw[i].astype(F32)
    rest[4][...]=output[...]
    rest[5][...]=gtok[...]


def widen(dup,ddown,dw,output,gtok,count=4):
    T,D=output.shape
    F=dup.shape[1]
    n=D//count
    rows=lambda r,c: pl.BlockSpec((r,c),lambda i:(i,0))
    sd=jax.ShapeDtypeStruct
    return pl.pallas_call(widen_kernel,grid=(count,),
        in_specs=[rows(n,F),rows(F//count,D),pl.BlockSpec((4,n,D),lambda i:(0,i,0)),rows(T//count,D),rows(T//count,D)],
        out_specs=[rows(n,F),rows(F//count,D)]+[rows(n,D)]*4+[rows(T//count,D)]*2,
        out_shape=[sd((D,F),F32),sd((F,D),F32)]+[sd((D,D),F32)]*4+[sd((T,D),BF),sd((T,D),F32)],
        compiler_params=pltpu.CompilerParams(vmem_limit_bytes=60*2**20),name="widen")(dup,ddown,dw,output,gtok)


EARLY=3
TILE_AT=(-1,-1,0,1,2,3,4,6,8,9)
RET_AT=(-1,-1,-1,-1,0,1,2)


def per_device(tokens,routes,gain_one,query_weight,key_weight,value_weight,out_weight,gain_two,up_weight,down_weight,cotangent):
    T,D=tokens.shape
    groups=lax.axis_size("expert")
    cap=2*T//groups
    g1=gain_one.reshape(1,D); g2=gain_two.reshape(1,D)
    weights=(query_weight,key_weight,value_weight,out_weight)
    normed,q,k,v,att,lse,hid,pack,slot,cotarr=front(tokens,routes.reshape(1,T),cotangent,g1,g2,*weights,groups,cap)
    gback,ret,chipu,chipd,xgot,_=expert(pack,cotarr,up_weight[0],down_weight[0],EARLY)
    output,gtok,dw,dgain,dup,ddown,_,_,_=back(gback,ret,slot,hid,cotangent,tokens,normed,q,k,v,att,lse,g1,g2,*weights,chipu,chipd,xgot,TILE_AT,RET_AT)
    gup,gdown,gq,gk,gv,go,output,gtok=widen(dup,ddown,dw,output,gtok)
    return (output,gtok,dgain[0],gq,gk,gv,go,dgain[1],gup[None],gdown[None])


def solution(mesh):
    rows=P(("expert","replica"),None)
    each=P("expert",None,None)
    return jax.shard_map(per_device,mesh=mesh,
        in_specs=(rows,rows,P(),P(),P(),P(),P(),P(),each,each,rows),
        out_specs=(rows,rows,P(),P(),P(),P(),P(),P(),each,each),check_vma=False)
```

```python
import functools
import math

import jax
import jax.numpy as jnp
from jax import lax
from jax.experimental import pallas as pl
from jax.experimental.pallas import tpu as pltpu
from jax.sharding import PartitionSpec as P

HEAD_DIM=64
F32=jnp.float32; BF=jnp.bfloat16
MESH=pl.DeviceIdType.MESH
epsilon=1e-5
def dot(a,b): return jnp.dot(a,b,preferred_element_type=F32)
def dg(a,b,ca,cb): return lax.dot_general(a,b,(((ca,),(cb,)),((),())),preferred_element_type=F32)

def xor(a,b,count):
    total=0; step=1
    while step<count:
        x=(a//step)%2; y=(b//step)%2
        total=total+step*(x+y-2*x*y); step*=2
    return total

def norm_stats(rows):
    average=jnp.mean(rows,axis=-1,keepdims=True)
    centred=rows-average
    inverse=lax.rsqrt(jnp.mean(centred*centred,axis=-1,keepdims=True)+epsilon)
    return centred*inverse,inverse

def fwd_head(qT,kT,vT,block):
    seq=qT.shape[1]
    qs=qT*jnp.asarray(HEAD_DIM**-0.5,BF)
    k=kT.T
    outs=[]; lses=[]
    for i in range(seq//block):
        b=i*block; n=b+block
        diag=dot(k[b:n],qs[:,b:n])
        rows=lax.broadcasted_iota(jnp.int32,(block,block),0); cols=lax.broadcasted_iota(jnp.int32,(block,block),1)
        diag=jnp.where(rows<=cols,diag,-1e30)
        m=jnp.max(diag,axis=0,keepdims=True)
        if i:
            s=dot(k[:b],qs[:,b:n])
            m=jnp.maximum(m,jnp.max(s,axis=0,keepdims=True))
        p=jnp.exp(diag-m)
        l=jnp.sum(p,axis=0,keepdims=True)
        o=dot(vT[:,b:n],p.astype(BF))
        if i:
            p=jnp.exp(s-m)
            l=l+jnp.sum(p,axis=0,keepdims=True)
            o=o+dot(vT[:,:b],p.astype(BF))
        outs.append((o*(1.0/l)).astype(BF)); lses.append(m+jnp.log(l))
    return outs,lses

def onehot_rows(slot,first,count):
    ids=(lax.broadcasted_iota(jnp.int32,(count,slot.shape[1]),0)+first).astype(F32)
    return jnp.where(ids==slot,1.0,0.0).astype(BF)

def front_kernel(groups,cap,block,htok,rt,cot,g1,g2,hwq,hwk,hwv,hwo,
                 hnormed,hq,hk,hv,hatt,lse,hhid,hpack,slot,cotarr,
                 tok,wq,wk,wv,wo,normed,q,k,v,att,hid,pack,cpack,n2,ssem,rsem,lsem,isem,osem):
    loads=[pltpu.make_async_copy(a,b,isem.at[i]) for i,(a,b) in enumerate(((htok,tok),(hwq,wq),(hwk,wk),(hwv,wv),(hwo,wo)))]
    for c in loads: c.start()
    stores=[pltpu.make_async_copy(a,b,osem.at[i]) for i,(a,b) in enumerate(((normed,hnormed),(q,hq),(k,hk),(v,hv),(att,hatt),(hid,hhid),(pack,hpack)))]
    T,D=tok.shape
    R=256
    me=lax.axis_index("expert")
    barrier=pltpu.get_barrier_semaphore()
    def greet(i,c):
        pl.semaphore_signal(barrier,inc=1,device_id={"expert":xor(me,i,groups)},device_id_type=MESH)
        return c
    lax.fori_loop(1,groups,greet,0)
    routes=rt[...]
    e=jnp.where(lax.broadcasted_iota(jnp.int32,(groups,T),0)==routes,1.0,0.0)
    tri=jnp.where(lax.broadcasted_iota(jnp.int32,(T,T),0)<=lax.broadcasted_iota(jnp.int32,(T,T),1),1.0,0.0).astype(BF)
    cum=dot(e.astype(BF),tri)
    rank=jnp.sum(cum*e,axis=0,keepdims=True)-1.0
    slots=routes.astype(F32)*cap+rank
    slot[...]=slots
    pl.semaphore_wait(barrier,groups-1)
    def push(i,c):
        peer=xor(me,groups-1-i,groups)
        cpack[peer]=dot(onehot_rows(slots,peer*cap,cap),cot[...]).astype(BF)
        pltpu.make_async_remote_copy(src_ref=cpack.at[peer],dst_ref=cotarr.at[me],send_sem=ssem.at[peer],recv_sem=rsem.at[me],
            device_id={"expert":peer},device_id_type=MESH).start()
        return c
    lax.fori_loop(0,groups-1,push,0)
    cpack[me]=dot(onehot_rows(slots,me*cap,cap),cot[...]).astype(BF)
    own=pltpu.make_async_copy(cpack.at[me],cotarr.at[me],lsem)
    own.start()
    for c in loads: c.wait()
    def norm_one(i,c):
        r=pl.ds(pl.multiple_of(i*R,R),R)
        u,_=norm_stats(tok[r,:].astype(F32))
        normed[:,r]=(u*g1[...]).astype(BF).T
        return c
    lax.fori_loop(0,T//R,norm_one,0)
    stores[0].start()
    def proj(i,c):
        s=pl.ds(pl.multiple_of(i*R,R),R)
        for w,o in ((wq,q),(wk,k),(wv,v)):
            o[s,:]=dg(w[:,s],normed[...],0,0).astype(BF)
        return c
    lax.fori_loop(0,D//R,proj,0)
    for c in stores[1:4]: c.start()
    def head(h,c):
        s=pl.ds(pl.multiple_of(h*HEAD_DIM,HEAD_DIM),HEAD_DIM)
        outs,lses=fwd_head(q[s,:],k[s,:],v[s,:],block)
        att[s,:]=jnp.concatenate(outs,axis=1)
        lse[pl.ds(h,1),:]=jnp.concatenate(lses,axis=1)
        return c
    lax.fori_loop(0,D//HEAD_DIM,head,0)
    stores[4].start()
    def out(i,c):
        r=pl.ds(pl.multiple_of(i*R,R),R)
        h=tok[r,:].astype(F32)+dg(att[:,r],wo[...],0,0)
        hid[r,:]=h
        u,_=norm_stats(h)
        n2[r,:]=(u*g2[...]).astype(BF)
        return c
    lax.fori_loop(0,T//R,out,0)
    stores[5].start()
    def packing(i,c):
        pack[i]=dot(onehot_rows(slots,i*cap,cap),n2[...]).astype(BF)
        return c
    lax.fori_loop(0,groups,packing,0)
    stores[6].start()
    own.wait()
    for c in stores: c.wait()
    def finish(i,c):
        peer=xor(me,i,groups)
        pltpu.make_async_remote_copy(src_ref=cpack.at[peer],dst_ref=cotarr.at[peer],send_sem=ssem.at[peer],recv_sem=rsem.at[peer],
            device_id={"expert":peer},device_id_type=MESH).wait()
        return c
    lax.fori_loop(1,groups,finish,0)

def front(tokens,routes_row,cot,g1,g2,wq,wk,wv,wo,groups,cap,block=512):
    T,D=tokens.shape
    H=D//HEAD_DIM
    V=pl.BlockSpec(memory_space=pltpu.VMEM)
    A=pl.BlockSpec(memory_space=pl.ANY)
    sd=jax.ShapeDtypeStruct
    return pl.pallas_call(functools.partial(front_kernel,groups,cap,block),
      in_specs=[A]+[V]*4+[A]*4,out_specs=[A]*5+[V]+[A]*2+[V,A],
      out_shape=[sd((D,T),BF)]*5+[sd((H,T),F32),sd((T,D),F32),sd((groups,cap,D),BF),sd((1,T),F32),sd((groups,cap,D),BF)],
      scratch_shapes=[pltpu.VMEM((T,D),BF)]+[pltpu.VMEM((D,D),BF)]*4+[pltpu.VMEM((D,T),BF)]*5+[pltpu.VMEM((T,D),F32),pltpu.VMEM((groups,cap,D),BF),pltpu.VMEM((groups,cap,D),BF),pltpu.VMEM((T,D),BF),pltpu.SemaphoreType.DMA((groups,)),pltpu.SemaphoreType.DMA((groups,)),pltpu.SemaphoreType.DMA,pltpu.SemaphoreType.DMA((5,)),pltpu.SemaphoreType.DMA((7,))],
      compiler_params=pltpu.CompilerParams(vmem_limit_bytes=60*2**20,collective_id=0,has_side_effects=True),
      name="front")(tokens,routes_row,cot,g1,g2,wq,wk,wv,wo)


F32=jnp.float32; BF=jnp.bfloat16
MESH=pl.DeviceIdType.MESH
def dot(a,b): return jnp.dot(a,b,preferred_element_type=F32)
def dg(a,b,ca,cb): return lax.dot_general(a,b,(((ca,),(cb,)),((),())),preferred_element_type=F32)
def xor(a,b,count):
    total=0; step=1
    while step<count:
        x=(a//step)%2; y=(b//step)%2
        total=total+step*(x+y-2*x*y); step*=2
    return total
SQ=math.sqrt(2/math.pi)
def gelu_pair(h):
    h2=h*h
    th=jnp.tanh(h*(SQ+SQ*0.044715*h2))
    half=0.5*(1.0+th)
    act=h*half
    slope=half+act*((1.0-th)*(SQ+3*SQ*0.044715*h2))
    return act,slope

def expert_kernel(groups,cap,early,pack,cotarr,up,down,gback,ret,chipu,chipd,xgot,act,
                  arr,upv,downv,cotv,gpre,actb,gst,retb,landu,landd,
                  psend,precv,gsend,grecv,wsem,retsem,actsem,tsem,ssend,srecv,xsend,xrecv,csem):
    rows=groups*cap
    D,F=upv.shape
    FT=1024
    me=lax.axis_index("expert")
    barrier=pltpu.get_barrier_semaphore()
    def greet(i,c):
        pl.semaphore_signal(barrier,inc=1,device_id={"expert":xor(me,i,groups)},device_id_type=MESH)
        return c
    lax.fori_loop(1,groups,greet,0)
    mine=lax.axis_index("replica")
    core=mine%2
    sibling=xor(mine,1,4); across=xor(mine,2,4)
    for peer in (sibling,across):
        pl.semaphore_signal(barrier,inc=1,device_id={"replica":peer},device_id_type=MESH)
    pl.semaphore_wait(barrier,groups+1)
    def at(j): return pl.ds(pl.multiple_of(j*cap,cap),cap)
    def dispatch(j,i):
        return pltpu.make_async_remote_copy(src_ref=pack.at[j],dst_ref=arr.at[at(me)],send_sem=psend.at[i],recv_sem=precv.at[i],
            device_id={"expert":j},device_id_type=MESH)
    def giveback(j,i):
        return pltpu.make_async_remote_copy(src_ref=gst.at[at(j)],dst_ref=gback.at[me],send_sem=gsend.at[i],recv_sem=grecv.at[i],
            device_id={"expert":j},device_id_type=MESH)
    half=groups//2
    def code(i): return i+(i//half)*((i+half//2)%half+half-i)
    def push(i,c):
        dispatch(xor(me,code(i),groups),i).start()
        return c
    lax.fori_loop(half,half+half//2,push,0)
    lax.fori_loop(1,half,push,0)
    own=pltpu.make_async_copy(pack.at[me],arr.at[at(me)],precv.at[0])
    own.start()
    cup=pltpu.make_async_copy(up,upv,wsem.at[0]); cup.start()
    ccot=pltpu.make_async_copy(cotarr,cotv,wsem.at[1]); ccot.start()
    cdown=pltpu.make_async_copy(down,downv,wsem.at[2]); cdown.start()
    cup.wait(); ccot.wait(); cdown.wait()
    def retcopy(j): return pltpu.make_async_copy(retb,ret.at[j],retsem)
    def actcopy(j): return pltpu.make_async_copy(actb,act.at[at(j)],actsem)
    def results(j):
        retb[...]=dot(actb[...],downv[...]).astype(BF)
        retcopy(j).start()
    def answer(i,c):
        giveback(xor(me,code(i),groups),i).start()
        return c
    def chunk(i,c):
        j=xor(me,code(i),groups)
        @pl.when(i==0)
        def _(): own.wait()
        @pl.when(i>0)
        def _(): dispatch(j,i).wait_recv()
        @pl.when(i==half-2)
        def _(): lax.fori_loop(half+half//2,groups,push,0)
        @pl.when(i==groups-1)
        def _():
            lax.fori_loop(half,groups-1,answer,0)
            lax.fori_loop(1,half,answer,0)
        @pl.when(i>=1)
        def _(): actcopy(j).wait()
        def tile(t,c):
            s=pl.ds(pl.multiple_of(t*FT,FT),FT)
            h=dot(arr[at(j),:],upv[:,s])
            g=dg(cotv[j],downv[s,:],1,1)
            a,slope=gelu_pair(h)
            actb[:,s]=a.astype(BF)
            gpre[at(j),s]=(g*slope).astype(BF)
            return c
        lax.fori_loop(0,F//FT,tile,0)
        gst[at(j),:]=dg(gpre[at(j),:],upv[...],1,1).astype(BF)
        @pl.when(i==groups-1)
        def _(): giveback(j,i).start()
        @pl.when(i==0)
        def _(): pltpu.make_async_copy(gst.at[at(j)],gback.at[me],grecv.at[0]).start()
        actcopy(j).start()
        @pl.when((i>=1)&(i<groups-1))
        def _(): retcopy(j).wait()
        @pl.when(i<groups-1)
        def _(): results(j)
        return c
    lax.fori_loop(0,groups,chunk,0)
    actcopy(0).wait()
    def atile(t,b): return pltpu.make_async_copy(act.at[:,pl.ds(pl.multiple_of(t*D,D),D)],downv.at[pl.ds(b*rows,rows)],tsem.at[b])
    S=512
    steps=F//(2*S)
    def shared(n):
        first=n*steps
        chip,land=(chipu,landu) if n==0 else (chipd,landd)
        def place(kind,b):
            if n==0:
                return upv.at[:,pl.ds((2*kind+b)*S,S)]
            return upv.at[pl.ds(b*S,S),pl.ds(kind*D,D)]
        def product(t,ref):
            if n==0:
                def part(k,c):
                    r=pl.ds(pl.multiple_of(k*S,S),S)
                    ref[r,:]=dg(arr[:,r],gpre[:,pl.ds(pl.multiple_of(t*S,S),S)],0,0).astype(BF)
                    return c
                lax.fori_loop(0,D//S,part,0)
            else:
                tb=(t//2)%2; Q=S//2
                def part(k,c):
                    a=downv[pl.ds(pl.multiple_of(tb*rows,rows),rows),pl.ds(pl.multiple_of((t%2)*S+k*Q,Q),Q)]
                    ref[pl.ds(pl.multiple_of(k*Q,Q),Q),:]=dg(a,cotv[...].reshape(rows,D),0,0).astype(BF)
                    return c
                lax.fori_loop(0,2,part,0)
        def tosib(s,b):
            return pltpu.make_async_remote_copy(src_ref=place(0,b),dst_ref=land.at[s],send_sem=ssend.at[first+s],recv_sem=srecv.at[first+s],
                device_id={"replica":sibling},device_id_type=MESH)
        def tochip(s,b): return pltpu.make_async_copy(place(1,b),chip.at[s],csem.at[first+s])
        def finish(s):
            tosib(s,s%2).wait_recv()
            ref=place(1,s%2)
            def add(k,c):
                r=pl.ds(pl.multiple_of(k*128,128),128)
                ref[r,:]=(ref[r,:].astype(F32)+land[s,r,:].astype(F32)).astype(BF)
                return c
            lax.fori_loop(0,ref.shape[0]//128,add,0)
            tochip(s,s%2).start()
        def leave(s):
            tochip(s,s%2).wait()
            if first+s<early: toacross(s).start()
        for s in range(steps):
            b=s%2
            if n==1: atile(s,b).wait()
            if s>=2: tosib(s-2,b).wait_send()
            product(2*s+1-core,place(0,b))
            tosib(s,b).start()
            if s>=2: finish(s-1)
            product(2*s+core,place(1,b))
            if n==1 and s+2<steps: atile(s+2,b).start()
            if s==0: finish(0)
            if s!=1: leave(max(s-1,0))
        finish(steps-1)
        for s in range(max(0,steps-2),steps): tosib(s,s%2).wait_send()
        leave(steps-1)
    def toacross(s):
        return pltpu.make_async_remote_copy(src_ref=chipu.at[s],dst_ref=xgot.at[s],send_sem=xsend.at[s],recv_sem=xrecv.at[s],
            device_id={"replica":across},device_id_type=MESH)
    shared(0)
    retcopy(0).wait()
    results(xor(me,code(groups-1),groups))
    retcopy(0).wait()
    atile(0,0).start(); atile(1,1).start()
    shared(1)
    pltpu.make_async_copy(gst.at[at(me)],gback.at[me],grecv.at[0]).wait()
    def finish(i,c):
        j=xor(me,code(i),groups)
        dispatch(j,i).wait_send()
        giveback(j,i).wait()
        return c
    lax.fori_loop(1,groups,finish,0)
    for s in range(early): toacross(s).wait()

def expert(pack,cotarr,up,down,early):
    groups,cap,D=pack.shape
    F=up.shape[1]; rows=groups*cap
    S=512; steps=F//(2*S)
    A=pl.BlockSpec(memory_space=pl.ANY)
    sd=jax.ShapeDtypeStruct
    DMA=pltpu.SemaphoreType.DMA
    su=sd((steps,D,S),BF); sdn=sd((steps,S,D),BF)
    return pl.pallas_call(functools.partial(expert_kernel,groups,cap,early),
      in_specs=[A]*4,out_specs=[A]*6,
      out_shape=[sd((groups,cap,D),BF)]*2+[su,sdn,sd((early,D,S),BF),sd((rows,F),BF)],
      scratch_shapes=[pltpu.VMEM((rows,D),BF),pltpu.VMEM((D,F),BF),pltpu.VMEM((F,D),BF),pltpu.VMEM((groups,cap,D),BF),pltpu.VMEM((rows,F),BF),
         pltpu.VMEM((cap,F),BF),pltpu.VMEM((rows,D),BF),pltpu.VMEM((cap,D),BF),pltpu.VMEM((steps,D,S),BF),pltpu.VMEM((steps,S,D),BF),
         DMA((groups,)),DMA((groups,)),DMA((groups,)),DMA((groups,)),DMA((3,)),DMA,DMA,DMA((2,)),
         DMA((2*steps,)),DMA((2*steps,)),DMA((early,)),DMA((early,)),DMA((2*steps,))],
      compiler_params=pltpu.CompilerParams(vmem_limit_bytes=63*2**20+2**19,collective_id=1,has_side_effects=True),
      name="experts")(pack,cotarr,up,down)


def bwd_head(qT,kT,vT,oT,doT,lse,block):
    seq=qT.shape[1]
    scale=HEAD_DIM**-0.5
    qs=qT*jnp.asarray(scale,BF)
    q=qs.T; k=kT.T; v=vT.T; do=doT.T
    delta=jnp.sum(oT.astype(F32)*doT.astype(F32),axis=0,keepdims=True)
    count=seq//block
    dqs=[None]*count; dks=[]; dvs=[]
    for j in range(count):
        b=j*block
        kj=k[b:b+block]; vj=v[b:b+block]
        s=dot(kj,qs[:,b:])
        n=seq-b
        rows=lax.broadcasted_iota(jnp.int32,(block,n),0); cols=lax.broadcasted_iota(jnp.int32,(block,n),1)
        p=jnp.where(rows<=cols,jnp.exp(s-lse[:,b:]),0.0)
        dp=dot(vj,doT[:,b:])
        ds=(p*(dp-delta[:,b:])).astype(BF)
        dvs.append(dot(p.astype(BF),do[b:]))
        dks.append(dot(ds,q[b:]))
        c=dot(kT[:,b:b+block],ds)
        for i in range(j,count):
            part=c[:,(i-j)*block:(i-j+1)*block]
            dqs[i]=part if dqs[i] is None else dqs[i]+part
    return [(x*scale).astype(BF).T for x in dqs],[x.astype(BF) for x in dks],[x.astype(BF) for x in dvs]

def back_kernel(groups,cap,block,early,tile_at,ret_at,
        gback,ret,slot,hid,cot,tok,normed,q,k,v,att,lse,g1,g2,wq,wk,wv,wo,chipu,chipd,xgot,
        output,gtok,dw,dgain,dup,ddown,rarr,xu,xd,
        vslots,vhid,vcot,vnormed,vq,vk,vv,vatt,vwo,ghl,datt,dq,dk,dv,vgt,dwv,rbuf,gbuf,
        isem,ssem,rsem,lsem,dsend,drecv,osem,xsend,xrecv,fsem,fout,fsend,frecv,gsend,grecv,credit):
    D,T=vnormed.shape
    R=256
    S=chipu.shape[2]
    steps=chipu.shape[0]
    parts=4
    W=D//parts
    rows=groups*cap
    me=lax.axis_index("expert")
    mine=lax.axis_index("replica")
    core=mine%2
    sibling=xor(mine,1,4); across=xor(mine,2,4)
    barrier=pltpu.get_barrier_semaphore()
    def greet(i,c):
        pl.semaphore_signal(barrier,inc=1,device_id={"expert":xor(me,i,groups)},device_id_type=MESH)
        return c
    lax.fori_loop(1,groups,greet,0)
    for peer in (sibling,across):
        pl.semaphore_signal(barrier,inc=1,device_id={"replica":peer},device_id_type=MESH)
    copies=[pltpu.make_async_copy(a,b,isem.at[i]) for i,(a,b) in enumerate(
        ((gback,vslots),(hid,vhid),(cot,vcot),(wo,vwo),(att,vatt),(q,vq),(k,vk),(v,vv),(normed,vnormed)))]
    for c in copies: c.start()
    pl.semaphore_wait(barrier,groups+1)
    def send(i):
        j=xor(me,i,groups)
        return pltpu.make_async_remote_copy(src_ref=ret.at[j],dst_ref=rarr.at[me],send_sem=ssem.at[i],recv_sem=rsem.at[i],
            device_id={"expert":j},device_id_type=MESH)
    def push(i,c):
        send(i).start()
        return c
    def push_share(p):
        lax.fori_loop(1+p*(groups-1)//7,1+(p+1)*(groups-1)//7,push,0)
    for p in range(7):
        if ret_at[p]<0: push_share(p)
    own=pltpu.make_async_copy(ret.at[me],rarr.at[me],lsem); own.start()
    def toacross(n,s,p):
        src,dst=(chipu.at[s],xu.at[s-early]) if n==0 else (chipd.at[s],xd.at[s])
        m=src.shape[0]//2
        return pltpu.make_async_remote_copy(src_ref=src.at[pl.ds(p*m,m)],dst_ref=dst.at[pl.ds(p*m,m)],send_sem=xsend.at[n,2*s+p],recv_sem=xrecv.at[n,2*s+p],
            device_id={"replica":across},device_id_type=MESH)
    late=[(n,s,p) for n in range(2) for s in range(0 if n else early,steps) for p in range(2)]
    def spare(n,i):
        return vatt.at[:,pl.ds(i*S,S)] if n==0 else vnormed.at[pl.ds(i*S,S)]
    def finalize(n,s,got):
        a,b=spare(n,0),spare(n,1)
        l1=pltpu.make_async_copy((chipu if n==0 else chipd).at[s],a,fsem.at[0]); l1.start()
        l2=pltpu.make_async_copy(got,b,fsem.at[1]); l2.start()
        l1.wait(); l2.wait()
        def add(i,c):
            r=pl.ds(pl.multiple_of(i*128,128),128)
            a[r,:]=(a[r,:].astype(F32)+b[r,:].astype(F32)).astype(BF)
            return c
        lax.fori_loop(0,a.shape[0]//128,add,0)
        keep,share=leaving(n,s)
        keep.start(); share.start()
    def leaving(n,s):
        a=spare(n,0)
        d=pl.ds(pl.multiple_of((2*s+core)*S,S),S)
        there=dup.at[:,d] if n==0 else ddown.at[d]
        return (pltpu.make_async_copy(a,there,fout.at[n]),
            pltpu.make_async_remote_copy(src_ref=a,dst_ref=there,send_sem=fsend.at[n,s],recv_sem=frecv.at[n,s],
                device_id={"replica":sibling},device_id_type=MESH))
    def left(n,s):
        keep,share=leaving(n,s)
        keep.wait(); share.wait_send()
    for i,x in enumerate(late):
        if tile_at[i]<0: toacross(*x).start()
    V=W//2
    half=[(1<<b) for b in range(groups.bit_length()-1)]
    def partner(index,step): return index+step-2*step*((index//step)%2)
    paths=[]
    for steps_of in (half[:-1],half[1::-1]+half[2:-1] if len(half)>2 else half[:-1]):
        base=[0]; other=[]; peers=[]
        for i,(axis,index,step) in enumerate([("replica",mine,1)]+[("expert",me,b) for b in steps_of]):
            n=D>>(i+1)
            bit=(index//step)%2
            other.append(base[-1]+(1-bit)*n)
            base.append(base[-1]+bit*n)
            peers.append({axis:partner(index,step)})
        paths.append((base,other,peers))
    whole=[{"expert":partner(me,half[-1])},{"replica":across}]
    H=len(paths[0][2])
    size=[D>>(i+1) for i in range(H)]+[D>>H]*2
    offset=[D-(D>>i) for i in range(H+1)]+[D]
    def columns(c,h): return pl.ds(pl.multiple_of(c*W+h*V,V),V)
    def piece(ref,c,h,first,n):
        return ref.at[2*c+h,:,pl.ds(pl.multiple_of(first,n),n),:]
    def move(c,h,k):
        base,other,peers=paths[h]
        if k<H:
            src=piece(dwv,c,h,other[k],size[k]); dst=piece(rbuf,c,h,offset[k],size[k]); peer=peers[k]
        elif k<H+2:
            src=piece(dwv,c,h,base[H],size[k]); dst=piece(rbuf,c,h,offset[k],size[k]); peer=whole[k-H]
        else:
            i=2*H+1-k
            src=dst=piece(dwv,c,h,base[i+1],size[i]); peer=peers[i]
        return pltpu.make_async_remote_copy(src_ref=src,dst_ref=dst,send_sem=dsend.at[2*c+h,k],recv_sem=drecv.at[2*c+h,k],device_id=peer,device_id_type=MESH)
    def gather_in(c,h,k):
        first=paths[h][0][min(k+1,H)]; n=size[k]
        m=min(n,64)
        lane=2*c+h
        def add(i,z):
            r=pl.ds(pl.multiple_of(first+i*m,m),m)
            o=pl.ds(pl.multiple_of(offset[k]+i*m,m),m)
            for x in range(4):
                dwv[lane,x,r,:]=(dwv[lane,x,r,:].astype(F32)+rbuf[lane,x,o,:].astype(F32)).astype(BF)
            return z
        lax.fori_loop(0,n//m,add,0)
    def out_dense(c,h):
        return pltpu.make_async_copy(dwv.at[2*c+h],dw.at[:,:,columns(c,h)],osem.at[2*c+h])
    K=2*H+3
    last=parts+K-1
    def progress(t):
        for k in [x for x in range(K-1,-1,-1) if x!=H+2]+[H+2]:
            c=t-k
            @pl.when((c>=0)&(c<parts))
            def _():
                for h in range(2):
                    if k>0:
                        move(c,h,k-1).wait()
                        if k<=H: pl.semaphore_signal(credit.at[2*c+h,k-1],inc=1,device_id=paths[h][2][k-1],device_id_type=MESH)
                    if 0<k<=H+2: gather_in(c,h,k-1)
                    if H+2<=k<K-1: pl.semaphore_wait(credit.at[2*c+h,2*H+1-k],1)
                    if k<K-1: move(c,h,k).start()
                    if k==K-1: out_dense(c,h).start()
    gbits=paths[0][2]+whole
    def gain_move(j):
        return pltpu.make_async_remote_copy(src_ref=dgain,dst_ref=gbuf.at[j],send_sem=gsend.at[j],recv_sem=grecv.at[j],device_id=gbits[j],device_id_type=MESH)
    def gain_step(j):
        if j>0:
            gain_move(j-1).wait()
            dgain[...]=dgain[...]+gbuf[j-1]
        if j<len(gbits): gain_move(j).start()
    def gathered(r):
        col=jnp.broadcast_to(slot[:,r],(128,R)).T[:,:1]
        ids=lax.broadcasted_iota(jnp.int32,(R,rows),1).astype(F32)
        return dot(jnp.where(ids==col,1.0,0.0).astype(BF),vslots[...].reshape(rows,D))
    for c in copies[:3]: c.wait()
    dgain[...]=jnp.zeros_like(dgain)
    def norm_two(i,c):
        r=pl.ds(pl.multiple_of(i*R,R),R)
        gs=gathered(r)
        u,inv=norm_stats(vhid[r,:])
        m=gs*g2[...]
        dgain[1:2,:]+=jnp.sum(gs*u,axis=0,keepdims=True)
        gh=vcot[r,:].astype(F32)+inv*(m-jnp.mean(m,axis=-1,keepdims=True)-u*jnp.mean(m*u,axis=-1,keepdims=True))
        vgt[r,:]=gh
        ghl[r,:]=gh.astype(BF)
        return c
    lax.fori_loop(0,T//R,norm_two,0)
    again=pltpu.make_async_copy(tok,vcot,isem.at[2]); again.start()
    for c in copies[3:5]: c.wait()
    def outproj(i,c):
        s=pl.ds(pl.multiple_of(i*R,R),R)
        datt[s,:]=dg(vwo[s,:],ghl[...],1,1).astype(BF)
        full=dot(vatt[s,:],ghl[...]).astype(BF)
        for x in range(2*parts): dwv[x,3,s,:]=full[:,x*V:(x+1)*V]
        return c
    lax.fori_loop(0,D//R,outproj,0)
    for c in copies[5:]: c.wait()
    w=2*HEAD_DIM
    def pair(h):
        col=pl.ds(pl.multiple_of(h*w,w),w)
        res=[]
        for a in range(2):
            s=pl.ds(pl.multiple_of(h*w+a*HEAD_DIM,HEAD_DIM),HEAD_DIM)
            res.append(bwd_head(vq[s,:],vk[s,:],vv[s,:],vatt[s,:],datt[s,:],lse[pl.ds(2*h+a,1),:],block))
        for ref,x,y in zip((dq,dk,dv),*res):
            for i in range(T//block):
                ref[i*block:(i+1)*block,col]=jnp.concatenate([x[i],y[i]],axis=1)
    loads=[pltpu.make_async_copy(a,b,isem.at[5+i]) for i,(a,b) in enumerate(((wq,vq),(wk,vk),(wv,vv)))]
    def time(t,c):
        @pl.when(t<parts)
        def _():
            per=D//w//parts
            def one(i,c):
                pair(t*per+i)
                return c
            lax.fori_loop(0,per,one,0)
            cols=pl.ds(pl.multiple_of(t*W,W),W)
            for n,x in enumerate((dq,dk,dv)):
                def rowpart(i,c):
                    s=pl.ds(pl.multiple_of(i*2*R,2*R),2*R)
                    full=dot(vnormed[s,:],x[:,cols]).astype(BF)
                    for h in range(2): dwv[2*t+h,n,s,:]=full[:,h*V:(h+1)*V]
                    return c
                lax.fori_loop(0,D//(2*R),rowpart,0)
        @pl.when(t==parts-1)
        def _():
            for x in loads: x.start()
        @pl.when(t==parts)
        def _():
            again.wait()
            for x in loads: x.wait()
        @pl.when((t>=parts)&(t<2*parts))
        def _():
            n=T//parts
            r=pl.ds(pl.multiple_of((t-parts)*n,n),n)
            gn=dg(dq[r,:],vq[...],1,1)+dg(dk[r,:],vk[...],1,1)+dg(dv[r,:],vv[...],1,1)
            u,inv=norm_stats(vcot[r,:].astype(F32))
            m=gn*g1[...]
            dgain[0:1,:]+=jnp.sum(gn*u,axis=0,keepdims=True)
            vgt[r,:]+=inv*(m-jnp.mean(m,axis=-1,keepdims=True)-u*jnp.mean(m*u,axis=-1,keepdims=True))
        progress(t)
        for at in range(last):
            if at in tile_at or at in ret_at:
                @pl.when(t==at)
                def _():
                    for i,x in enumerate(late):
                        if tile_at[i]==at: toacross(*x).start()
                    for p in range(7):
                        if ret_at[p]==at: push_share(p)
        @pl.when(t==2*parts)
        def _(): pltpu.make_async_copy(vgt,gtok,isem.at[0]).start()
        @pl.when(t==2*parts)
        def _(): returned()
        @pl.when((t>=2*parts)&(t<3*parts))
        def _(): final(t-2*parts)
        for j in range(ingain):
            @pl.when(t==2*parts-1+j)
            def _(): gain_step(j)
        for p,(n,s) in enumerate(order[:inloop]):
            @pl.when(t==parts+p)
            def _(): settle(p)
        return c
    def returned():
        own.wait()
        def finish(i,c):
            send(i).wait()
            return c
        lax.fori_loop(1,groups,finish,0)
        load=pltpu.make_async_copy(rarr,vslots,lsem); load.start(); load.wait()
    def final(i):
        n=T//parts
        r=pl.ds(pl.multiple_of(i*n,n),n)
        ghl[r,:]=(vhid[r,:]+gathered(r)).astype(BF)
    order=[(0,s) for s in range(steps)]+[(1,s) for s in range(steps)]
    def settle(p):
        n,s=order[p]
        if p>0 and order[p-1][0]==n: left(n,s-1)
        if n==0 and s<early:
            finalize(n,s,xgot.at[s])
        else:
            for i in range(2): toacross(n,s,i).wait()
            finalize(n,s,xu.at[s-early] if n==0 else xd.at[s])
        if p>0 and order[p-1][0]!=n: left(*order[p-1])
    inloop=min(2*steps,last-parts)
    ingain=min(len(gbits)+1,last-2*parts+1)
    lax.fori_loop(0,last,time,0)
    for j in range(ingain,len(gbits)+1): gain_step(j)
    for p in range(inloop,len(order)): settle(p)
    last_out=pltpu.make_async_copy(ghl,output,isem.at[1]); last_out.start()
    left(*order[-1])
    for n,s in order: leaving(n,s)[1].wait_recv()
    for c in range(parts):
        for h in range(2): out_dense(c,h).wait()
    pltpu.make_async_copy(vgt,gtok,isem.at[0]).wait()
    last_out.wait()

def back(gback,ret,slot,hid,cot,tok,normed,q,k,v,att,lse,g1,g2,wq,wk,wv,wo,chipu,chipd,xgot,tile_at,ret_at,block=256):
    groups,cap,D=ret.shape
    T=tok.shape[0]
    steps,_,S=chipu.shape
    early=xgot.shape[0]
    F=2*steps*S
    H=groups.bit_length()-1
    V=pl.BlockSpec(memory_space=pltpu.VMEM)
    A=pl.BlockSpec(memory_space=pl.ANY)
    sd=jax.ShapeDtypeStruct
    DMA=pltpu.SemaphoreType.DMA
    M=lambda *s: pltpu.VMEM(s,BF)
    return pl.pallas_call(functools.partial(back_kernel,groups,cap,block,early,tile_at,ret_at),
      in_specs=[A,A,V]+[A]*8+[V]*3+[A]*7,out_specs=[A]*3+[V]+[A]*5,
      out_shape=[sd((T,D),BF),sd((T,D),F32),sd((4,D,D),BF),sd((8,D),F32),sd((D,F),BF),sd((F,D),BF),sd((groups,cap,D),BF),
         sd((steps-early,D,S),BF),sd((steps,S,D),BF)],
      scratch_shapes=[M(groups,cap,D),pltpu.VMEM((T,D),F32),M(T,D),M(D,T),M(D,T),M(D,T),M(D,T),M(D,T),M(D,D),M(T,D),M(D,T),M(T,D),M(T,D),M(T,D),
         pltpu.VMEM((T,D),F32),M(8,4,D,D//8),M(8,4,D+(D>>H),D//8),pltpu.VMEM((H+2,8,D),F32),
         DMA((9,)),DMA((groups,)),DMA((groups,)),DMA,DMA((8,2*H+2)),DMA((8,2*H+2)),DMA((8,)),DMA((2,2*steps)),DMA((2,2*steps)),DMA((2,)),DMA((2,)),DMA((2,steps)),DMA((2,steps)),
         DMA((H+2,)),DMA((H+2,)),pltpu.SemaphoreType.REGULAR((8,H))],
      compiler_params=pltpu.CompilerParams(vmem_limit_bytes=63*2**20+2**19,collective_id=2,has_side_effects=True),
      name="back")(gback,ret,slot,hid,cot,tok,normed,q,k,v,att,lse,g1,g2,wq,wk,wv,wo,chipu,chipd,xgot)


def widen_kernel(dup,ddown,dw,output,gtok,gup,gdown,*rest):
    gup[...]=dup[...].astype(F32)
    gdown[...]=ddown[...].astype(F32)
    for i in range(4): rest[i][...]=dw[i].astype(F32)
    rest[4][...]=output[...]
    rest[5][...]=gtok[...]


def widen(dup,ddown,dw,output,gtok,count=4):
    T,D=output.shape
    F=dup.shape[1]
    n=D//count
    rows=lambda r,c: pl.BlockSpec((r,c),lambda i:(i,0))
    sd=jax.ShapeDtypeStruct
    return pl.pallas_call(widen_kernel,grid=(count,),
        in_specs=[rows(n,F),rows(F//count,D),pl.BlockSpec((4,n,D),lambda i:(0,i,0)),rows(T//count,D),rows(T//count,D)],
        out_specs=[rows(n,F),rows(F//count,D)]+[rows(n,D)]*4+[rows(T//count,D)]*2,
        out_shape=[sd((D,F),F32),sd((F,D),F32)]+[sd((D,D),F32)]*4+[sd((T,D),BF),sd((T,D),F32)],
        compiler_params=pltpu.CompilerParams(vmem_limit_bytes=60*2**20),name="widen")(dup,ddown,dw,output,gtok)


EARLY=3
TILE_AT=(-1,-1,0,1,2,3,5,6,7,8)
RET_AT=(-1,-1,-1,0,1,3,5)


def per_device(tokens,routes,gain_one,query_weight,key_weight,value_weight,out_weight,gain_two,up_weight,down_weight,cotangent):
    T,D=tokens.shape
    groups=lax.axis_size("expert")
    cap=2*T//groups
    g1=gain_one.reshape(1,D); g2=gain_two.reshape(1,D)
    weights=(query_weight,key_weight,value_weight,out_weight)
    normed,q,k,v,att,lse,hid,pack,slot,cotarr=front(tokens,routes.reshape(1,T),cotangent,g1,g2,*weights,groups,cap)
    gback,ret,chipu,chipd,xgot,_=expert(pack,cotarr,up_weight[0],down_weight[0],EARLY)
    output,gtok,dw,dgain,dup,ddown,_,_,_=back(gback,ret,slot,hid,cotangent,tokens,normed,q,k,v,att,lse,g1,g2,*weights,chipu,chipd,xgot,TILE_AT,RET_AT)
    gup,gdown,gq,gk,gv,go,output,gtok=widen(dup,ddown,dw,output,gtok)
    return (output,gtok,dgain[0],gq,gk,gv,go,dgain[1],gup[None],gdown[None])


def solution(mesh):
    rows=P(("expert","replica"),None)
    each=P("expert",None,None)
    return jax.shard_map(per_device,mesh=mesh,
        in_specs=(rows,rows,P(),P(),P(),P(),P(),P(),each,each,rows),
        out_specs=(rows,rows,P(),P(),P(),P(),P(),P(),each,each),check_vma=False)
```
